128 devices in a mesh: tmpl: 16 (over z, y), seg: 8 (over x, core).
Axes of the slice: x: 4, y: 4, z: 4, core: 2. Of those that a mesh axis runs over, the one named last changes fastest.
Arguments:
- strain: bfloat16 [2, 2, 8, 512, 1024], P(None, None, 'seg', 'tmpl'), may hold values from -6 to 6
- templates: bfloat16 [2, 16, 512, 1024], P(None, 'tmpl', 'seg'), may hold values from -400 to 400
- trig_pair: int32 [128, 256], P(('tmpl', 'seg')), may hold values from 0 to 127, as said below
- trig_time: int32 [128, 256], P(('tmpl', 'seg')), may hold values from 0 to 524287
- trig_counts: int32 [128], P(('tmpl', 'seg')), may hold values from 128 to 256, as said below
Outputs:
- snr_series: float32 [16, 8, 1024, 512], P('tmpl', 'seg')
- peak: float32 [16, 8], P('tmpl', 'seg')
- chi_square: float32 [128, 256], P(('tmpl', 'seg'))
- trigger_snr: float32 [128, 256], P(('tmpl', 'seg'))
The draws below stay inside these ranges and needn't reach their ends.
Inputs may be any that keep to these rules, and one draw needn't show every extreme that they name: `trig_pair`: among the live rows of one device's list no value appears more than 2 times, and one value, the same for every device, appears exactly 2 times in every device's live rows. `trig_counts`: some device's list is live in full.
All inputs are finite; a program needn't handle non-finite values.
Results may differ from the reference program's by a relative error of at most 0.0055.
Values may be sent and summed in bfloat16 or wider, within the bound.
No kernel may reach another device: no remote copies, remote signals or barrier semaphores. Data moves between devices by JAX's collectives and lax.ppermute only.
A program may use at most 64 MiB of HBM per device.

```python
import math
import jax
import jax.numpy as jnp
from jax import lax

N1 = 512
N2 = 1024
TSAMP = 524288
DETECTORS = 2
BANDS = 16
KDEV = 256
TEMPLATES = 16
SEGS = 8
MOST = 2


def live_counts(key):
    pair_total = TEMPLATES * SEGS
    counts = jax.random.randint(jax.random.fold_in(key, 41), (pair_total,), KDEV // 2, KDEV + 1)
    full_row = jax.random.randint(jax.random.fold_in(key, 42), (), 0, pair_total)
    return jnp.where(jnp.arange(pair_total) == full_row, KDEV, counts).astype(jnp.int32)


def draw_trig_counts(key, part):
    counts = live_counts(key)
    return counts


def draw_trig_pair(key, part):
    counts = live_counts(key)
    key = jax.random.fold_in(key, 5)
    pair_total = TEMPLATES * SEGS
    hot_pair = jax.random.randint(jax.random.fold_in(key, 1), (), 0, pair_total)
    list_keys = jax.random.split(jax.random.fold_in(key, 2), pair_total)

    def one_list(list_key, live_total):
        rounds = jax.random.split(list_key, MOST + 1)
        others = jax.vmap(lambda round_key: jax.random.permutation(round_key, pair_total - 1))(rounds[:MOST])
        others = (hot_pair + 1 + others) % pair_total
        sequence = jnp.concatenate([jnp.full((MOST,), hot_pair, jnp.int32), others.reshape(-1).astype(jnp.int32)])
        positions = jnp.arange(KDEV, dtype=jnp.int32)
        scores = jnp.where(positions < live_total, jax.random.permutation(rounds[MOST], KDEV).astype(jnp.int32), KDEV + positions)
        return sequence[jnp.argsort(scores, stable=True)]
    return jax.vmap(one_list)(list_keys, counts).astype(jnp.int32)


def draw_templates(key, part):
    key = jax.random.fold_in(key, 7)
    full_shape = (2, TEMPLATES, N1, N2)
    row_scale = jnp.exp(math.log(10.0) * jax.random.uniform(jax.random.fold_in(key, 1), (1, TEMPLATES, N1, 1), jnp.float32))
    col_scale = jnp.exp(math.log(10.0) * jax.random.uniform(jax.random.fold_in(key, 2), (1, TEMPLATES, 1, N2), jnp.float32))
    base = jax.random.truncated_normal(jax.random.fold_in(key, 3), -4.0, 4.0, full_shape, jnp.float32)
    return (base * row_scale * col_scale).astype(jnp.bfloat16)


def set_ends(entries, own_key, least, high):
    index_at = [jax.random.randint(jax.random.fold_in(own_key, axis), (), 0, length) for axis, length in enumerate(entries.shape)]
    widest = entries.shape.index(max(entries.shape))
    neighbour = index_at[:widest] + [(index_at[widest] + 1) % entries.shape[widest]] + index_at[widest + 1:]
    return entries.at[tuple(index_at)].set(least).at[tuple(neighbour)].set(high)


def block_levels(stream_key, extent, cuts, smallest, top_value):
    gain, own = 1.0, jax.random.fold_in(stream_key, 6)
    for dim, shards_of in cuts:
        heights = jnp.exp(jax.random.uniform(jax.random.fold_in(own, dim), (shards_of,), jnp.float32, smallest / len(cuts), top_value / len(cuts)))
        gain = gain * jnp.repeat(heights, extent[dim] // shards_of).reshape([-1 if axis == dim else 1 for axis in range(len(extent))])
    return gain


def bell_draw(stream_key, dims, width, bound, pieces=(), held_as=jnp.bfloat16):
    loudness = block_levels(stream_key, dims, pieces, -0.22, 0.18) if pieces else 1.0
    entries = jax.random.normal(stream_key, dims, jnp.float32) * width * loudness
    return jnp.minimum(jnp.maximum(entries, -bound), bound).astype(held_as)


def setup_inputs(seed: int = 0) -> dict:
    keys = jax.random.split(jax.random.key(seed), 6)
    strain = bell_draw(keys[0], (2, DETECTORS, SEGS, N1, N2), 1.0, 6.0, ((2, 8), (3, 16)))
    templates = draw_templates(jax.random.fold_in(keys[5], 71), 0)
    trig_pair = draw_trig_pair(jax.random.fold_in(keys[5], 71), 0)
    trig_time = set_ends(jax.random.randint(keys[3], (TEMPLATES * SEGS, KDEV), 0, TSAMP), jax.random.fold_in(keys[3], 1), 0, TSAMP - 1).astype(jnp.int32)
    trig_counts = draw_trig_counts(jax.random.fold_in(keys[5], 71), 0)
    return dict(strain=strain, templates=templates, trig_pair=trig_pair, trig_time=trig_time, trig_counts=trig_counts)


def phase_parts(numerator, modulus):
    angles = (2.0 * math.pi / modulus) * (numerator % modulus).astype(jnp.float32)
    return jnp.cos(angles), jnp.sin(angles)


def as_float(values):
    return values.astype(jnp.float32)


def complex_product(form, left_real, left_imag, right_real, right_imag):
    highest = lax.Precision.HIGHEST
    real_part = jnp.einsum(form, as_float(left_real), as_float(right_real), precision=highest) - jnp.einsum(form, as_float(left_imag), as_float(right_imag), precision=highest)
    imag_part = jnp.einsum(form, as_float(left_real), as_float(right_imag), precision=highest) + jnp.einsum(form, as_float(left_imag), as_float(right_real), precision=highest)
    return real_part, imag_part


def fourier_tables():
    row_index = jnp.arange(N1, dtype=jnp.int32)
    col_index = jnp.arange(N2, dtype=jnp.int32)
    outer_real, outer_imag = phase_parts(row_index[:, None] * row_index[None, :], N1)
    inner_real, inner_imag = phase_parts(col_index[:, None] * col_index[None, :], N2)
    twiddle_real, twiddle_imag = phase_parts(row_index[:, None] * col_index[None, :], TSAMP)
    return (outer_real.astype(jnp.bfloat16), outer_imag.astype(jnp.bfloat16), inner_real.astype(jnp.bfloat16), inner_imag.astype(jnp.bfloat16), twiddle_real, twiddle_imag)


def veto_terms(spec_real, spec_imag, row_power, sigma_sq, sample_times):
    row_index = jnp.arange(N1, dtype=jnp.int32)
    col_index = jnp.arange(N2, dtype=jnp.int32)
    probe_real, probe_imag = phase_parts(col_index[:, None] * sample_times[None, :], TSAMP)
    band_real, band_imag = complex_product("dac,ck->dak", spec_real, spec_imag, probe_real.astype(jnp.bfloat16), probe_imag.astype(jnp.bfloat16))
    shift_real, shift_imag = phase_parts(row_index[:, None] * sample_times[None, :], N1)
    moved_real = band_real * shift_real - band_imag * shift_imag
    moved_imag = band_real * shift_imag + band_imag * shift_real
    sums_real = moved_real.reshape(DETECTORS, BANDS, N1 // BANDS, -1).sum(axis=2)
    sums_imag = moved_imag.reshape(DETECTORS, BANDS, N1 // BANDS, -1).sum(axis=2)
    total_real = sums_real.sum(axis=1)
    total_imag = sums_imag.sum(axis=1)
    weights = row_power.reshape(BANDS, -1).sum(axis=1) / sigma_sq
    diff_real = sums_real - weights[None, :, None] * total_real[:, None, :]
    diff_imag = sums_imag - weights[None, :, None] * total_imag[:, None, :]
    chi_terms = (diff_real * diff_real + diff_imag * diff_imag) / (weights[None, :, None] * sigma_sq)
    chi_value = chi_terms.sum(axis=(0, 1)) / (4.0 * (BANDS - 1))
    snr_value = (total_real * total_real + total_imag * total_imag).sum(axis=0) / (2.0 * sigma_sq)
    return chi_value, snr_value


def reference(strain, templates, trig_pair, trig_time, trig_counts):
    outer_real, outer_imag, inner_real, inner_imag, twiddle_real, twiddle_imag = fourier_tables()
    pair_total = TEMPLATES * SEGS
    flat_pairs = trig_pair.reshape(-1)
    flat_times = trig_time.reshape(-1)
    slot_index = jnp.arange(KDEV, dtype=jnp.int32)
    live_rows = (slot_index[None, :] < trig_counts[:, None]).reshape(-1)

    def pair_work(pair_id):
        tmpl_id = pair_id // SEGS
        seg_id = pair_id % SEGS
        bank = lax.dynamic_index_in_dim(templates, tmpl_id, 1, keepdims=False)
        data = lax.dynamic_index_in_dim(strain, seg_id, 2, keepdims=False)
        tmpl_real = as_float(bank[0])
        tmpl_imag = as_float(bank[1])
        data_real = as_float(data[0])
        data_imag = as_float(data[1])
        spec_real = (tmpl_real * data_real + tmpl_imag * data_imag).astype(jnp.bfloat16)
        spec_imag = (tmpl_real * data_imag - tmpl_imag * data_real).astype(jnp.bfloat16)
        row_power = jnp.sum(tmpl_real * tmpl_real + tmpl_imag * tmpl_imag, axis=1)
        sigma_sq = jnp.sum(row_power)
        first_real, first_imag = complex_product("ta,dac->dtc", outer_real, outer_imag, spec_real, spec_imag)
        turned_real = (first_real * twiddle_real - first_imag * twiddle_imag).astype(jnp.bfloat16)
        turned_imag = (first_real * twiddle_imag + first_imag * twiddle_real).astype(jnp.bfloat16)
        final_real, final_imag = complex_product("cu,dtc->dut", inner_real, inner_imag, turned_real, turned_imag)
        series = jnp.sum(final_real * final_real + final_imag * final_imag, axis=0) / (2.0 * sigma_sq)
        chosen = (flat_pairs == pair_id) & live_rows
        picked = jnp.nonzero(chosen, size=KDEV, fill_value=0)[0].astype(jnp.int32)
        usable = slot_index < jnp.sum(chosen.astype(jnp.int32))
        chi_value, snr_value = veto_terms(spec_real, spec_imag, row_power, sigma_sq, flat_times[picked])
        return series, jnp.max(series), picked, jnp.where(usable, chi_value, 0.0), jnp.where(usable, snr_value, 0.0)

    series, peaks, picked, chi_all, snr_all = lax.map(pair_work, jnp.arange(pair_total, dtype=jnp.int32))
    snr_series = series.reshape(TEMPLATES, SEGS, N2, N1)
    peak = peaks.reshape(TEMPLATES, SEGS)
    chi_square = jnp.zeros((pair_total * KDEV,), jnp.float32).at[picked.reshape(-1)].add(chi_all.reshape(-1)).reshape(pair_total, KDEV)
    trigger_snr = jnp.zeros((pair_total * KDEV,), jnp.float32).at[picked.reshape(-1)].add(snr_all.reshape(-1)).reshape(pair_total, KDEV)
    return (snr_series, peak, chi_square, trigger_snr)
```

```python
import functools
import math

import jax
import jax.numpy as jnp
import numpy as np
import ml_dtypes
from jax import lax
from jax.experimental import pallas as pl
from jax.experimental.pallas import tpu as pltpu
from jax.sharding import PartitionSpec as P

BANDS = 16
ROWS = 512
COLS = 1024
BINS = ROWS * COLS
BLOCK = 32
SLOTS = 256
OFFSETS = (0, 3, 1, 2)
F32 = jnp.float32
BF16 = jnp.bfloat16
VMEM = pl.BlockSpec(memory_space=pltpu.VMEM)
SMEM = pl.BlockSpec(memory_space=pltpu.SMEM)
LIMIT = 48 * 1024 * 1024


def unit(numerator, modulus):
    angle = 2.0 * math.pi * (np.asarray(numerator, np.int64) % modulus) / modulus
    return np.cos(angle), np.sin(angle)


def row_matrices():
    out = np.zeros((4, 4, 256, 256), np.float32)
    u = np.arange(128)
    for y in range(4):
        a = np.concatenate([32 * ((y + o) % 4) + np.arange(32) for o in OFFSETS])
        for p in range(4):
            c, s = unit(a[None, :] * (4 * u[:, None] + p), ROWS)
            out[y, p] = np.block([[c, -s], [s, c]])
    return out.astype(ml_dtypes.bfloat16)


def col_matrices():
    out = np.zeros((4, 512, 512), np.float32)
    n = np.arange(256)
    for p in range(4):
        c, s = unit(n[:, None] * (4 * n[None, :] + p), COLS)
        out[p] = np.block([[c, s], [-s, c]])
    return out.astype(ml_dtypes.bfloat16)


def twiddles():
    out = np.zeros((4, 2, 128, COLS), np.float32)
    u = np.arange(128)
    for p in range(4):
        c, s = unit((4 * u[:, None] + p) * np.arange(COLS)[None, :], BINS)
        out[p, 0], out[p, 1] = c, s
    return out


def along_tmpl(x, dz, dy):
    pairs = [
        (z * 4 + y, ((z + dz) % 4) * 4 + (y + dy) % 4) for z in range(4) for y in range(4)
    ]
    return lax.ppermute(x, "tmpl", pairs)


def along_seg(x, dx, dc):
    pairs = [(k * 2 + c, ((k + dx) % 4) * 2 + (c + dc) % 2) for k in range(4) for c in range(2)]
    return lax.ppermute(x, "seg", pairs)


def angle_parts(numerator, modulus):
    angles = (2.0 * math.pi / modulus) * (numerator & (modulus - 1)).astype(F32)
    return jnp.cos(angles), jnp.sin(angles)


def probe_kernel(time_ref, one_ref, two_ref, shift_ref, band_ref):
    t = jnp.maximum(time_ref[...], 0)
    step = lax.broadcasted_iota(jnp.int32, (32, SLOTS), 0)
    low_r, low_i = angle_parts(step * t, BINS)
    high_r, high_i = angle_parts(step * 32 * t, BINS)
    shift_ref[0], shift_ref[1] = angle_parts(step * t, ROWS)
    band_ref[0], band_ref[1] = angle_parts(step[:BANDS] * t, BANDS)
    for h in range(32):
        hr, hi = high_r[h : h + 1], high_i[h : h + 1]
        pr = (hr * low_r - hi * low_i).astype(BF16)
        pi = (hr * low_i + hi * low_r).astype(BF16)
        rows = pl.ds(32 * h, 32)
        one_ref[rows, :SLOTS] = pr
        one_ref[rows, SLOTS:] = pi
        two_ref[rows, :SLOTS] = -pi
        two_ref[rows, SLOTS:] = pr


def probes(times):
    return pl.pallas_call(
        probe_kernel,
        out_shape=(
            jax.ShapeDtypeStruct((COLS, 2 * SLOTS), BF16),
            jax.ShapeDtypeStruct((COLS, 2 * SLOTS), BF16),
            jax.ShapeDtypeStruct((2, 32, SLOTS), F32),
            jax.ShapeDtypeStruct((2, BANDS, SLOTS), F32),
        ),
        in_specs=[VMEM],
        out_specs=(VMEM,) * 4,
        compiler_params=pltpu.CompilerParams(vmem_limit_bytes=LIMIT),
        cost_estimate=pl.CostEstimate(flops=4_000_000, bytes_accessed=2_200_000, transcendentals=60_000),
        name="probes",
    )(times)


def veto_kernel(zones, prior, final, *refs):
    n = len(zones)
    place, own_ref, other_ref, one_ref, two_ref, shift_ref, band_ref = refs[:7]
    parts = refs[7 : 7 + 2 * n]
    refs = refs[7 + 2 * n :]
    before = refs[: 2 * prior]
    refs = refs[2 * prior :]
    if final:
        time_ref, refs = refs[0], refs[1:]
    specs, refs = refs[:n], refs[n:]
    if final:
        result_ref, sigma_ref, sum_ref, power_ref = refs
    else:
        sum_ref, power_ref = refs
    z, y, x, core = place[0], place[1], place[2], place[3]
    sr, si = shift_ref[0], shift_ref[1]

    def block_place(det, zone, m):
        om = jnp.where(m == 0, 0, jnp.where(m == 1, 3, m - 1))
        oz, oy = (OFFSETS[zone], om) if det == 0 else (om, OFFSETS[zone])
        return (z + oz) & 3, (y + oy) & 3

    for index, zone in enumerate(zones):
        spec = specs[index]
        for det in range(2):
            part = parts[2 * index + det]

            def one_block(m, carry, det=det, part=part, zone=zone, spec=spec, index=index):
                zz, yy = block_place(det, zone, m)
                rel = (zz - x) & 3
                pos = jnp.where(rel == 0, 0, jnp.where(rel == 3, 1, rel + 1))
                mine = (yy >> 1) == core
                rows = pl.ds(pl.multiple_of(32 * (yy & 1), 32), 32)
                total = jnp.zeros((8, 128), F32)
                for lane in range(0, COLS, 256):
                    cols = pl.ds(lane, 256)
                    h = [
                        jnp.where(
                            mine,
                            own_ref[pos, k, rows, cols].astype(F32),
                            other_ref[pos, k, rows, cols].astype(F32),
                        )
                        for k in range(2)
                    ]
                    xr = part[m, 0, :, cols].astype(F32)
                    xi = part[m, 1, :, cols].astype(F32)
                    spec[0, 4 * det + m, :, cols] = (h[0] * xr + h[1] * xi).astype(BF16)
                    spec[1, 4 * det + m, :, cols] = (h[0] * xi - h[1] * xr).astype(BF16)
                    power = h[0] * h[0] + h[1] * h[1]
                    for r in range(0, 32, 8):
                        for c in range(0, 256, 128):
                            total = total + power[r : r + 8, c : c + 128]
                whole = jnp.sum(total, axis=(0, 1), keepdims=True)
                power_ref[pl.ds(8 * index + 4 * det + m, 1), :] = jnp.broadcast_to(whole, (1, SLOTS))
                return carry

            lax.fori_loop(0, 4, one_block, 0)
        out = jnp.dot(spec[0].reshape(256, COLS), one_ref[...], preferred_element_type=F32)
        out = out + jnp.dot(spec[1].reshape(256, COLS), two_ref[...], preferred_element_type=F32)
        for det in range(2):
            for m in range(4):
                i = 4 * det + m
                yr = out[32 * i : 32 * i + 32, :SLOTS]
                yi = out[32 * i : 32 * i + 32, SLOTS:]
                ar = jnp.sum(yr * sr - yi * si, axis=0, keepdims=True)
                ai = jnp.sum(yr * si + yi * sr, axis=0, keepdims=True)
                zz, yy = block_place(det, zone, m)
                band = 4 * zz + yy
                er = band_ref[0, pl.ds(band, 1), :]
                ei = band_ref[1, pl.ds(band, 1), :]
                sum_ref[8 * index + i : 8 * index + i + 1, :SLOTS] = ar * er - ai * ei
                sum_ref[8 * index + i : 8 * index + i + 1, SLOTS:] = ar * ei + ai * er
    if not final:
        return
    sums = [before[2 * k][...] for k in range(prior)] + [sum_ref[...]]
    powers = [before[2 * k + 1][...] for k in range(prior)] + [power_ref[...]]
    sums = jnp.concatenate(sums, axis=0)
    powers = jnp.concatenate(powers, axis=0)
    groups = sums.shape[0] // 8
    per_det = []
    for det in range(2):
        pick = lambda v: jnp.concatenate(
            [v[8 * g + 4 * det : 8 * g + 4 * det + 4] for g in range(groups)], axis=0
        )
        per_det.append((pick(sums), pick(powers)))
    sigma = jnp.sum(per_det[0][1], axis=0, keepdims=True)
    chi = jnp.zeros((1, SLOTS), F32)
    snr = jnp.zeros((1, SLOTS), F32)
    for both, power in per_det:
        br, bi = both[:, :SLOTS], both[:, SLOTS:]
        tr = jnp.sum(br, axis=0, keepdims=True)
        ti = jnp.sum(bi, axis=0, keepdims=True)
        weight = power / sigma
        dr = br - weight * tr
        di = bi - weight * ti
        chi = chi + jnp.sum((dr * dr + di * di) / (weight * sigma), axis=0, keepdims=True)
        snr = snr + (tr * tr + ti * ti)
    usable = time_ref[...] >= 0
    result_ref[0:1, :] = jnp.where(usable, chi / (4.0 * (BANDS - 1)), 0.0)
    result_ref[1:2, :] = jnp.where(usable, snr / (2.0 * sigma), 0.0)
    sigma_ref[...] = sigma


def veto(zones, place, own, other, tables, parts, before=(), times=None):
    n = len(zones)
    final = times is not None
    inputs = [place, own, other, *tables, *parts, *before] + ([times] if final else [])
    specs = [jax.ShapeDtypeStruct((2, 8, 32, COLS), BF16)] * n
    sums = [
        jax.ShapeDtypeStruct((8 * n, 2 * SLOTS), F32),
        jax.ShapeDtypeStruct((8 * n, SLOTS), F32),
    ]
    if final:
        outs = specs + [
            jax.ShapeDtypeStruct((2, SLOTS), F32),
            jax.ShapeDtypeStruct((1, SLOTS), F32),
        ]
        scratch = [pltpu.VMEM(s.shape, s.dtype) for s in sums]
    else:
        outs = specs + sums
        scratch = []
    return pl.pallas_call(
        functools.partial(veto_kernel, zones, len(before) // 2, final),
        out_shape=tuple(outs),
        in_specs=[SMEM] + [VMEM] * (len(inputs) - 1),
        out_specs=(VMEM,) * len(outs),
        scratch_shapes=scratch,
        compiler_params=pltpu.CompilerParams(vmem_limit_bytes=LIMIT),
        cost_estimate=pl.CostEstimate(
            flops=n * 560_000_000, bytes_accessed=n * 2_000_000 + 4_000_000, transcendentals=0
        ),
        name="veto_last" if final else "veto_part",
    )(*inputs)


def series_kernel(s0, s1, s2, s3, rows_ref, turn_ref, cols_ref, sigma_ref, out_ref, peak_ref, x_ref, w_ref, t_ref, o_ref):
    specs = (s0, s1, s2, s3)

    def four(q):
        (r0, i0), (r3, i3), (r1, i1), (r2, i2) = q
        ar, ai = r0 + r2, i0 + i2
        br, bi = r1 + r3, i1 + i3
        cr, ci = r0 - r2, i0 - i2
        dr, di = r1 - r3, i1 - i3
        return (
            (ar + br, ai + bi),
            (cr - di, ci + dr),
            (ar - br, ai - bi),
            (cr + di, ci - dr),
        )

    def fold(det, m, load):
        def chunk(k, carry):
            cols = pl.ds(pl.multiple_of(k * 256, 256), 256)
            q = [(load(o, 0, cols).astype(F32), load(o, 1, cols).astype(F32)) for o in range(4)]
            for p, (re, im) in enumerate(four(q)):
                x_ref[det, p, pl.ds(32 * m, 32), cols] = re.astype(BF16)
                x_ref[det, p, pl.ds(128 + 32 * m, 32), cols] = im.astype(BF16)
            return carry

        lax.fori_loop(0, 4, chunk, 0)

    for m in range(4):
        fold(0, m, lambda o, part, cols: specs[o][part, m, :, cols])
        fold(1, m, lambda o, part, cols: specs[m][part, 4 + o, :, cols])

    def first(step, carry):
        det = step // 4
        p = step % 4
        matrix = rows_ref[p]
        h = []
        for j in range(4):
            cols = pl.ds(256 * j, 256)
            g = jnp.dot(matrix, x_ref[det, p, :, cols], preferred_element_type=F32)
            gr, gi = g[:128], g[128:]
            tr = turn_ref[p, 0, :, cols]
            ti = turn_ref[p, 1, :, cols]
            h.append((gr * tr - gi * ti, gr * ti + gi * tr))
        (r0, i0), (r1, i1), (r2, i2), (r3, i3) = h
        for k, (re, im) in enumerate(four(((r0, i0), (r3, i3), (r1, i1), (r2, i2)))):
            rows = pl.ds(pl.multiple_of(128 * p, 128), 128)
            w_ref[k, det, rows, :256] = re.astype(BF16)
            w_ref[k, det, rows, 256:] = im.astype(BF16)
        return carry

    lax.fori_loop(0, 8, first, 0)

    scale = 1.0 / (2.0 * sigma_ref[0, 0])

    def second(k, best):
        total = None
        for det in range(2):
            out = jnp.dot(w_ref[k, det], cols_ref[k], preferred_element_type=F32)
            re, im = out[:, :256], out[:, 256:]
            power = re * re + im * im
            total = power if total is None else total + power
        total = total * scale
        for p in range(4):
            for half in range(2):
                t_ref[2 * k + half, pl.ds(p, 128, stride=4), :] = total[
                    128 * p : 128 * p + 128, 128 * half : 128 * half + 128
                ]
        best = jnp.maximum(best, jnp.max(total.reshape(64, 8, 256), axis=0))
        return best

    best = lax.fori_loop(0, 4, second, jnp.zeros((8, 256), F32))
    peak_ref[...] = jnp.max(best, axis=(0, 1), keepdims=True)
    for k in range(4):
        for half in range(2):
            for i in range(4):
                tile = t_ref[2 * k + half, pl.ds(128 * i, 128), :]
                o_ref[i, pl.ds(512 * half + k, 128, stride=4), :] = tile.T
    for i in range(4):
        out_ref[:, pl.ds(128 * i, 128)] = o_ref[i]


def series(specs, rows, turns, cols, sigma):
    return pl.pallas_call(
        series_kernel,
        out_shape=(
            jax.ShapeDtypeStruct((COLS, ROWS), F32),
            jax.ShapeDtypeStruct((1, 1), F32),
        ),
        in_specs=[VMEM] * 8,
        out_specs=(VMEM, VMEM),
        scratch_shapes=[
            pltpu.VMEM((2, 4, 256, COLS), BF16),
            pltpu.VMEM((4, 2, ROWS, 512), BF16),
            pltpu.VMEM((8, ROWS, 128), F32),
            pltpu.VMEM((4, COLS, 128), F32),
        ],
        compiler_params=pltpu.CompilerParams(vmem_limit_bytes=LIMIT),
        cost_estimate=pl.CostEstimate(
            flops=3_300_000_000, bytes_accessed=13_000_000, transcendentals=0
        ),
        name="series",
    )(*specs, rows, turns, cols, sigma)


def shards(strain, templates, trig_pair, trig_time, trig_counts):
    device = lax.axis_index("tmpl")
    seat = lax.axis_index("seg")
    place = jnp.stack([device // 4, device % 4, seat // 2, seat % 2]).astype(jnp.int32)
    rows = lax.dynamic_index_in_dim(jnp.asarray(row_matrices()), device % 4, 0, keepdims=False)
    turns = jnp.asarray(twiddles())
    cols = jnp.asarray(col_matrices())

    a, b, t = strain[:, 0, 0], strain[:, 1, 0], templates[:, 0]
    a = [a, along_tmpl(a, 0, 1), along_tmpl(a, 0, 3), along_tmpl(a, 0, 2)]
    b = [b, along_tmpl(b, 1, 0), along_tmpl(b, 3, 0), along_tmpl(b, 2, 0)]
    t = [t, along_seg(t, 1, 0), along_seg(t, 3, 0), along_seg(t, 2, 0)]
    a, b, t = jnp.stack(a), jnp.stack(b), jnp.stack(t)
    a = [a, along_tmpl(a, 1, 0), along_tmpl(a, 3, 0), along_tmpl(a, 2, 0)]
    b = [b, along_tmpl(b, 0, 1), along_tmpl(b, 0, 3), along_tmpl(b, 0, 2)]
    other = along_seg(t, 0, 1)

    device_total = lax.axis_size("tmpl") * lax.axis_size("seg")
    pair_list = trig_pair[0]
    time_list = trig_time[0]
    slots_each = SLOTS // device_total
    positions = jnp.arange(SLOTS, dtype=jnp.int32)
    live_rows = positions < trig_counts[0]
    same = (pair_list[:, None] == pair_list[None, :]) & (positions[None, :] < positions[:, None])
    slot_rank = jnp.sum((same & live_rows[None, :]).astype(jnp.int32), axis=1)
    slot_of = pair_list * slots_each + slot_rank
    slot_match = (slot_of[:, None] == positions[None, :]) & live_rows[:, None]
    outgoing = jnp.sum(jnp.where(slot_match, time_list[:, None] + 1, 0), axis=0) - 1
    incoming = lax.all_to_all(
        outgoing.reshape(device_total, slots_each),
        ("tmpl", "seg"),
        split_axis=0,
        concat_axis=0,
        tiled=True,
    )
    times = incoming.reshape(1, SLOTS)
    tables = probes(times)
    spec0, sum0, power0 = veto((0,), place, t, other, tables, (a[0], b[0]))
    parts = [v for k in (1, 2, 3) for v in (a[k], b[k])]
    *rest, result, sigma = veto((1, 2, 3), place, t, other, tables, parts, (sum0, power0), times)
    back = lax.all_to_all(
        result.reshape(2, device_total, slots_each),
        ("tmpl", "seg"),
        split_axis=1,
        concat_axis=1,
        tiled=True,
    ).reshape(2, SLOTS)
    snr_series, peak = series((spec0, *rest), rows, turns, cols, sigma)
    mine = jnp.sum(jnp.where(slot_match[None], back[:, None, :], 0.0), axis=2)
    return (snr_series[None, None], peak, mine[0][None], mine[1][None])


def solution(mesh):
    in_specs = (
        P(None, None, "seg", "tmpl", None),
        P(None, "tmpl", "seg", None),
        P(("tmpl", "seg"), None),
        P(("tmpl", "seg"), None),
        P(("tmpl", "seg")),
    )
    out_specs = (
        P("tmpl", "seg", None, None),
        P("tmpl", "seg"),
        P(("tmpl", "seg"), None),
        P(("tmpl", "seg"), None),
    )
    return jax.shard_map(shards, mesh=mesh, in_specs=in_specs, out_specs=out_specs, check_vma=False)
```

```python
import functools
import math

import jax
import jax.numpy as jnp
import numpy as np
import ml_dtypes
from jax import lax
from jax.experimental import pallas as pl
from jax.experimental.pallas import tpu as pltpu
from jax.sharding import PartitionSpec as P

BANDS = 16
ROWS = 512
COLS = 1024
BINS = ROWS * COLS
BLOCK = 32
SLOTS = 256
PAIRS = 128
F32 = jnp.float32
BF16 = jnp.bfloat16
VMEM = pl.BlockSpec(memory_space=pltpu.VMEM)
SMEM = pl.BlockSpec(memory_space=pltpu.SMEM)
LIMIT = 48 * 1024 * 1024


def unit(numerator, modulus):
    angle = 2.0 * math.pi * (np.asarray(numerator, np.int64) % modulus) / modulus
    return np.cos(angle), np.sin(angle)


def row_matrices():
    out = np.zeros((4, 256, 256), np.float32)
    n = np.arange(128)
    for p in range(4):
        c, s = unit(n[None, :] * (4 * n[:, None] + p), ROWS)
        out[p] = np.block([[c, -s], [s, c]])
    return out.astype(ml_dtypes.bfloat16)


def col_matrices():
    out = np.zeros((4, 512, 512), np.float32)
    n = np.arange(256)
    for p in range(4):
        c, s = unit(n[:, None] * (4 * n[None, :] + p), COLS)
        out[p] = np.block([[c, s], [-s, c]])
    return out.astype(ml_dtypes.bfloat16)


def twiddles():
    out = np.zeros((4, 2, 128, COLS), np.float32)
    u = np.arange(128)
    for p in range(4):
        c, s = unit((4 * u[:, None] + p) * np.arange(COLS)[None, :], BINS)
        out[p, 0], out[p, 1] = c, s
    return out


def swap(x, *moves):
    pairs = []
    for z in range(4):
        for y in range(4):
            for k in range(4):
                for core in range(2):
                    axis, mask = moves[core]
                    to = {
                        "z": (z ^ mask, y, k, core),
                        "y": (z, y ^ mask, k, core),
                        "x": (z, y, k ^ mask, core),
                        "core": (z, y, k, core ^ mask),
                    }[axis]
                    number = lambda v: ((v[0] * 4 + v[1]) * 4 + v[2]) * 2 + v[3]
                    pairs.append((number((z, y, k, core)), number(to)))
    return lax.ppermute(x, ("tmpl", "seg"), pairs)


def distance(position, swapped):
    apart = position ^ (position >> 1)
    return jnp.where(swapped, (4 - apart) & 3, apart)


def order_kernel(place, own_ref, other_ref, out_ref, power_ref):
    x, core = place[2], place[3]
    for turned, ref in enumerate((own_ref, other_ref)):
        holder = core ^ turned

        def one(position, carry, ref=ref, holder=holder):
            rank = 2 * (x ^ distance(position, holder == 1)) + holder
            for half in range(2):
                total = jnp.zeros((8, 128), F32)
                for part in range(2):
                    h = ref[position, part, pl.ds(32 * half, 32), :]
                    out_ref[part, pl.ds(pl.multiple_of(64 * rank + 32 * half, 32), 32), :] = h
                    h = h.astype(F32)
                    power = h * h
                    for r in range(0, 32, 8):
                        for c in range(0, COLS, 128):
                            total = total + power[r : r + 8, c : c + 128]
                whole = jnp.sum(total, axis=(0, 1), keepdims=True)
                power_ref[pl.ds(2 * rank + half, 1), :] = jnp.broadcast_to(whole, (1, SLOTS))
            return carry

        lax.fori_loop(0, 4, one, 0)


def order_template(place, own, other):
    return pl.pallas_call(
        order_kernel,
        out_shape=(
            jax.ShapeDtypeStruct((2, ROWS, COLS), BF16),
            jax.ShapeDtypeStruct((BANDS, SLOTS), F32),
        ),
        in_specs=[SMEM, VMEM, VMEM],
        out_specs=(VMEM, VMEM),
        compiler_params=pltpu.CompilerParams(vmem_limit_bytes=12 * 1024 * 1024),
        cost_estimate=pl.CostEstimate(flops=3_000_000, bytes_accessed=4_000_000, transcendentals=0),
        name="order_template",
    )(place, own, other)


def list_masks(pair_ref, count_ref):
    shape = (PAIRS, SLOTS)
    row = lax.broadcasted_iota(jnp.int32, shape, 1).astype(F32)
    owner = lax.broadcasted_iota(jnp.int32, shape, 0)
    hit = (pair_ref[...] == owner) & (row < count_ref[0].astype(F32))
    low = jnp.min(jnp.where(hit, row, 1e6), axis=1, keepdims=True)
    high = jnp.max(jnp.where(hit, row, -1.0), axis=1, keepdims=True)
    return hit & (row == low), hit & (row == high) & (high > low)


def send_kernel(pair_ref, time_ref, count_ref, out_ref):
    times = time_ref[...].astype(F32) + 1.0
    lane = lax.broadcasted_iota(jnp.int32, (PAIRS, 128), 1)
    out = jnp.zeros((PAIRS, 128), F32)
    for slot, mask in enumerate(list_masks(pair_ref, count_ref)):
        value = jnp.sum(jnp.where(mask, times, 0.0), axis=1, keepdims=True)
        out = jnp.where(lane == slot, value, out)
    out_ref[...] = out.astype(jnp.int32) - 1


def send_lists(pairs, times, counts):
    return pl.pallas_call(
        send_kernel,
        out_shape=jax.ShapeDtypeStruct((PAIRS, 128), jnp.int32),
        in_specs=[VMEM, VMEM, SMEM],
        out_specs=VMEM,
        cost_estimate=pl.CostEstimate(flops=500_000, bytes_accessed=70_000, transcendentals=0),
        name="send_lists",
    )(pairs, times, counts)


def take_kernel(pair_ref, count_ref, back_ref, chi_ref, snr_ref):
    first, second = list_masks(pair_ref, count_ref)
    for part, out_ref in enumerate((chi_ref, snr_ref)):
        one = jnp.where(first, back_ref[:, 2 * part : 2 * part + 1], 0.0)
        two = jnp.where(second, back_ref[:, 2 * part + 1 : 2 * part + 2], 0.0)
        out_ref[...] = jnp.sum(one + two, axis=0, keepdims=True)


def take_results(pairs, counts, back):
    return pl.pallas_call(
        take_kernel,
        out_shape=(jax.ShapeDtypeStruct((1, SLOTS), F32),) * 2,
        in_specs=[VMEM, SMEM, VMEM],
        out_specs=(VMEM, VMEM),
        cost_estimate=pl.CostEstimate(flops=500_000, bytes_accessed=70_000, transcendentals=0),
        name="take_results",
    )(pairs, counts, back)


def angle_parts(numerator, modulus):
    angles = (2.0 * math.pi / modulus) * (numerator & (modulus - 1)).astype(F32)
    return jnp.cos(angles), jnp.sin(angles)


def probe_kernel(list_ref, one_ref, two_ref, shift_ref, band_ref, time_ref):
    lists = list_ref[...].astype(F32).T
    t = jnp.concatenate([lists[0:1], lists[1:2]], axis=1).astype(jnp.int32)
    time_ref[...] = t
    t = jnp.maximum(t, 0)
    step = lax.broadcasted_iota(jnp.int32, (32, SLOTS), 0)
    low_r, low_i = angle_parts(step * t, BINS)
    high_r, high_i = angle_parts(step * 32 * t, BINS)
    shift_ref[0], shift_ref[1] = angle_parts(step * t, ROWS)
    band_ref[0], band_ref[1] = angle_parts(step[:BANDS] * t, BANDS)
    for h in range(32):
        hr, hi = high_r[h : h + 1], high_i[h : h + 1]
        pr = (hr * low_r - hi * low_i).astype(BF16)
        pi = (hr * low_i + hi * low_r).astype(BF16)
        rows = pl.ds(32 * h, 32)
        one_ref[rows, :SLOTS] = pr
        one_ref[rows, SLOTS:] = pi
        two_ref[rows, :SLOTS] = -pi
        two_ref[rows, SLOTS:] = pr


def probes(lists):
    return pl.pallas_call(
        probe_kernel,
        out_shape=(
            jax.ShapeDtypeStruct((COLS, 2 * SLOTS), BF16),
            jax.ShapeDtypeStruct((COLS, 2 * SLOTS), BF16),
            jax.ShapeDtypeStruct((2, 32, SLOTS), F32),
            jax.ShapeDtypeStruct((2, BANDS, SLOTS), F32),
            jax.ShapeDtypeStruct((1, SLOTS), jnp.int32),
        ),
        in_specs=[VMEM],
        out_specs=(VMEM,) * 5,
        compiler_params=pltpu.CompilerParams(vmem_limit_bytes=LIMIT),
        cost_estimate=pl.CostEstimate(flops=4_000_000, bytes_accessed=2_200_000, transcendentals=60_000),
        name="probes",
    )(lists)


def block_place(place, det, late, early):
    z, y, core = place[0], place[1], place[3]
    late, early = distance(late, core == 1), distance(early, core == 1)
    return (z ^ late, y ^ early) if det == 0 else (z ^ early, y ^ late)


def spectra_kernel(half, place, template_ref, part0, part1, spec):
    for det, part in enumerate((part0, part1)):

        def one_block(m, carry, det=det, part=part):
            zz, yy = block_place(place, det, 2 * half + (m >> 2), m & 3)
            rows = pl.ds(pl.multiple_of(128 * zz + 32 * yy, 32), 32)
            for lane in range(0, COLS, 256):
                cols = pl.ds(lane, 256)
                hr = template_ref[0, rows, cols].astype(F32)
                hi = template_ref[1, rows, cols].astype(F32)
                xr = part[m, 0, :, cols].astype(F32)
                xi = part[m, 1, :, cols].astype(F32)
                spec[0, 8 * det + m, :, cols] = (hr * xr + hi * xi).astype(BF16)
                spec[1, 8 * det + m, :, cols] = (hr * xi - hi * xr).astype(BF16)
            return carry

        lax.fori_loop(0, 8, one_block, 0, unroll=2)


def spectra(half, place, template, parts):
    return pl.pallas_call(
        functools.partial(spectra_kernel, half),
        out_shape=jax.ShapeDtypeStruct((2, 16, 32, COLS), BF16),
        in_specs=[SMEM, VMEM, VMEM, VMEM],
        out_specs=VMEM,
        compiler_params=pltpu.CompilerParams(vmem_limit_bytes=12 * 1024 * 1024),
        cost_estimate=pl.CostEstimate(flops=3_000_000, bytes_accessed=6_000_000, transcendentals=0),
        name=("spectra_early", "spectra_late")[half],
    )(place, template, *parts)


def veto_kernel(place, power_ref, time_ref, one_ref, two_ref, shift_ref, band_ref, s0, s1, result_ref, sum_ref):
    sr, si = shift_ref[0], shift_ref[1]
    for half, spec in enumerate((s0, s1)):
        out = jnp.dot(spec[0].reshape(512, COLS), one_ref[...], preferred_element_type=F32)
        out = out + jnp.dot(spec[1].reshape(512, COLS), two_ref[...], preferred_element_type=F32)
        for det in range(2):
            for m in range(8):
                i = 8 * det + m
                yr = out[32 * i : 32 * i + 32, :SLOTS]
                yi = out[32 * i : 32 * i + 32, SLOTS:]
                ar = jnp.sum(yr * sr - yi * si, axis=0, keepdims=True)
                ai = jnp.sum(yr * si + yi * sr, axis=0, keepdims=True)
                zz, yy = block_place(place, det, 2 * half + (m >> 2), m & 3)
                band = 4 * zz + yy
                er = band_ref[0, pl.ds(band, 1), :]
                ei = band_ref[1, pl.ds(band, 1), :]
                sum_ref[pl.ds(BANDS * det + band, 1), :SLOTS] = ar * er - ai * ei
                sum_ref[pl.ds(BANDS * det + band, 1), SLOTS:] = ar * ei + ai * er
    power = power_ref[...]
    sigma = jnp.sum(power, axis=0, keepdims=True)
    weight = power / sigma
    chi = jnp.zeros((1, SLOTS), F32)
    snr = jnp.zeros((1, SLOTS), F32)
    for det in range(2):
        rows = pl.ds(BANDS * det, BANDS)
        br, bi = sum_ref[rows, :SLOTS], sum_ref[rows, SLOTS:]
        tr = jnp.sum(br, axis=0, keepdims=True)
        ti = jnp.sum(bi, axis=0, keepdims=True)
        dr = br - weight * tr
        di = bi - weight * ti
        chi = chi + jnp.sum((dr * dr + di * di) / (weight * sigma), axis=0, keepdims=True)
        snr = snr + (tr * tr + ti * ti)
    usable = time_ref[...] >= 0
    chi = jnp.where(usable, chi / (4.0 * (BANDS - 1)), 0.0)
    snr = jnp.where(usable, snr / (2.0 * sigma), 0.0)
    lines = [chi[:, :128], chi[:, 128:], snr[:, :128], snr[:, 128:], sigma[:, :128], jnp.zeros((123, 128), F32)]
    result_ref[...] = jnp.concatenate(lines, axis=0).T


def veto(place, power, times, tables, specs):
    return pl.pallas_call(
        veto_kernel,
        out_shape=jax.ShapeDtypeStruct((PAIRS, 128), F32),
        in_specs=[SMEM] + [VMEM] * 8,
        out_specs=VMEM,
        scratch_shapes=[pltpu.VMEM((2 * BANDS, 2 * SLOTS), F32)],
        compiler_params=pltpu.CompilerParams(vmem_limit_bytes=20 * 1024 * 1024),
        cost_estimate=pl.CostEstimate(
            flops=2_200_000_000, bytes_accessed=6_000_000, transcendentals=0
        ),
        name="veto",
    )(place, power, times, *tables, *specs)


def series_kernel(
    place, s0_hbm, s1_hbm, result_hbm, rows_hbm, turn_hbm, cols_hbm, out_ref, peak_ref,
    s0, s1, sigma_ref, rows_ref, turn_ref, cols_ref, x_ref, g_ref, w_ref, v_ref, t_ref, o_ref, sems,
):
    copies = [
        pltpu.make_async_copy(src, dst, sems.at[k])
        for k, (src, dst) in enumerate(
            (
                (s0_hbm.at[:, :8], s0.at[:, :8]),
                (s1_hbm.at[:, :8], s1.at[:, :8]),
                (s0_hbm.at[:, 8:], s0.at[:, 8:]),
                (s1_hbm.at[:, 8:], s1.at[:, 8:]),
                (rows_hbm, rows_ref),
                (turn_hbm, turn_ref),
                (cols_hbm, cols_ref),
                (result_hbm.at[:8], sigma_ref),
            )
        )
    ]
    for copy in copies:
        copy.start()
    specs = (s0, s1)
    z, y, core = place[0], place[1], place[3]

    def four(q):
        (r0, i0), (r1, i1), (r2, i2), (r3, i3) = q
        ar, ai = r0 + r2, i0 + i2
        br, bi = r1 + r3, i1 + i3
        cr, ci = r0 - r2, i0 - i2
        dr, di = r1 - r3, i1 - i3
        return (
            (ar + br, ai + bi),
            (cr - di, ci + dr),
            (ar - br, ai - bi),
            (cr + di, ci - dr),
        )

    turned = ((z & 1) ^ core) == 1

    def fold(det, yy, load):
        def chunk(k, carry):
            cols = pl.ds(pl.multiple_of(k * 256, 256), 256)
            q = [(load(o, 0, cols).astype(F32), load(o, 1, cols).astype(F32)) for o in (0, 1, 3, 2)]
            for p, (re, im) in enumerate(four(q)):
                to = jnp.where(turned, (4 - p) & 3, p)
                x_ref[det, to, pl.ds(pl.multiple_of(32 * yy, 32), 32), cols] = re.astype(BF16)
                x_ref[det, to, pl.ds(pl.multiple_of(128 + 32 * yy, 32), 32), cols] = im.astype(BF16)
            return carry

        lax.fori_loop(0, 4, chunk, 0)

    for det in range(2):
        copies[2 * det].wait()
        copies[2 * det + 1].wait()

        for m in range(4):
            if det == 0:
                load = lambda o, k, cols: specs[o >> 1][k, 4 * (o & 1) + m, :, cols]
            else:
                load = lambda o, k, cols: specs[m >> 1][k, 8 + 4 * (m & 1) + o, :, cols]
            fold(det, y ^ distance(m, core == 1), load)

    copies[4].wait()
    copies[5].wait()

    def first(step):
        g_ref[step % 2] = jnp.dot(
            rows_ref[step % 4], x_ref[step // 4, step % 4], preferred_element_type=F32
        )

    def turn(step):
        det, p = divmod(step, 4)
        for r in range(0, 128, 16):
            h = []
            for j in range(4):
                cols = pl.ds(256 * j, 256)
                gr = g_ref[step % 2, pl.ds(r, 16), cols]
                gi = g_ref[step % 2, pl.ds(128 + r, 16), cols]
                tr = turn_ref[p, 0, pl.ds(r, 16), cols]
                ti = turn_ref[p, 1, pl.ds(r, 16), cols]
                h.append((gr * tr - gi * ti, gr * ti + gi * tr))
            rows = pl.ds(128 * p + r, 16)
            for k, (re, im) in enumerate(four(h)):
                w_ref[k, det, rows, :256] = re.astype(BF16)
                w_ref[k, det, rows, 256:] = im.astype(BF16)

    first(0)
    for step in range(8):
        if step < 7:
            first(step + 1)
        turn(step)
    copies[6].wait()
    copies[7].wait()

    scale = 1.0 / (2.0 * sigma_ref[0, 4])

    def second(k):
        for det in range(2):
            v_ref[k % 2, det] = jnp.dot(w_ref[k, det], cols_ref[k], preferred_element_type=F32)

    def power(k, best):
        for p in range(4):
            for r in range(0, 128, 16):
                rows = pl.ds(128 * p + r, 16)
                v = [
                    v_ref[k % 2, det, rows, pl.ds(256 * part, 256)]
                    for det in range(2)
                    for part in range(2)
                ]
                total = (v[0] * v[0] + v[1] * v[1] + v[2] * v[2] + v[3] * v[3]) * scale
                best = jnp.maximum(best, jnp.maximum(total[:8], total[8:]))
                for half in range(2):
                    t_ref[2 * k + half, pl.ds(4 * r + p, 16, stride=4), :] = total[
                        :, 128 * half : 128 * half + 128
                    ]
        return best

    best = jnp.zeros((8, 256), F32)
    second(0)
    for k in range(4):
        if k < 3:
            second(k + 1)
        best = power(k, best)
    peak_ref[...] = jnp.max(best, axis=(0, 1), keepdims=True)
    for k in range(4):
        for half in range(2):
            for i in range(4):
                tile = t_ref[2 * k + half, pl.ds(128 * i, 128), :]
                o_ref[i, pl.ds(512 * half + k, 128, stride=4), :] = tile.T
    for i in range(4):
        out_ref[:, pl.ds(128 * i, 128)] = o_ref[i]


def series(place, specs, result, rows, turns, cols):
    hbm = pl.BlockSpec(memory_space=pltpu.HBM)
    return pl.pallas_call(
        series_kernel,
        out_shape=(
            jax.ShapeDtypeStruct((COLS, ROWS), F32),
            jax.ShapeDtypeStruct((1, 1), F32),
        ),
        in_specs=[SMEM] + [hbm] * 6,
        out_specs=(VMEM, VMEM),
        scratch_shapes=[
            pltpu.VMEM(specs[0].shape, BF16),
            pltpu.VMEM(specs[1].shape, BF16),
            pltpu.VMEM((8, 128), F32),
            pltpu.VMEM(rows.shape, rows.dtype),
            pltpu.VMEM(turns.shape, turns.dtype),
            pltpu.VMEM(cols.shape, cols.dtype),
            pltpu.VMEM((2, 4, 256, COLS), BF16),
            pltpu.VMEM((2, 256, COLS), F32),
            pltpu.VMEM((4, 2, ROWS, 512), BF16),
            pltpu.VMEM((2, 2, ROWS, 512), F32),
            pltpu.VMEM((8, ROWS, 128), F32),
            pltpu.VMEM((4, COLS, 128), F32),
            pltpu.SemaphoreType.DMA((8,)),
        ],
        compiler_params=pltpu.CompilerParams(vmem_limit_bytes=60 * 1024 * 1024),
        cost_estimate=pl.CostEstimate(
            flops=3_300_000_000, bytes_accessed=13_000_000, transcendentals=0
        ),
        name="series",
    )(place, *specs, result, rows, turns, cols)


def shards(strain, templates, trig_pair, trig_time, trig_counts):
    device = lax.axis_index("tmpl")
    seat = lax.axis_index("seg")
    place = jnp.stack([device // 4, device % 4, seat // 2, seat % 2]).astype(jnp.int32)

    a, b = strain[:, 0, 0][None], strain[:, 1, 0][None]
    t = templates[:, 0][None]
    outgoing = send_lists(trig_pair, trig_time, trig_counts)
    incoming = lax.all_to_all(
        outgoing, ("tmpl", "seg"), split_axis=0, concat_axis=0, tiled=True
    )
    for step, (near, far) in enumerate(((1, 3), (3, 1), (1, 3), (3, 1))):
        if step == 2:
            a, b, incoming = lax.optimization_barrier((a, b, incoming))
        more_a = swap(a, ("yyzz"[step], near), ("yyzz"[step], far))
        more_b = swap(b, ("zzyy"[step], near), ("zzyy"[step], far))
        if step < 2:
            t = jnp.concatenate([t, swap(t, ("x", near), ("x", far))])
        if step < 3:
            a, b = jnp.concatenate([a, more_a]), jnp.concatenate([b, more_b])
    other_t = swap(t, ("core", 1), ("core", 1))

    template, power = order_template(place, t, other_t)
    specs = spectra(0, place, template, (a, b)), spectra(1, place, template, (more_a, more_b))
    *tables, times = probes(incoming)
    result = veto(place, power, times, tables, specs)
    back = lax.all_to_all(result, ("tmpl", "seg"), split_axis=0, concat_axis=0, tiled=True)
    snr_series, peak = series(
        place,
        specs,
        result,
        jnp.asarray(row_matrices()),
        jnp.asarray(twiddles()),
        jnp.asarray(col_matrices()),
    )
    chi, snr = take_results(trig_pair, trig_counts, back)
    return (snr_series[None, None], peak, chi, snr)


def solution(mesh):
    in_specs = (
        P(None, None, "seg", "tmpl", None),
        P(None, "tmpl", "seg", None),
        P(("tmpl", "seg"), None),
        P(("tmpl", "seg"), None),
        P(("tmpl", "seg")),
    )
    out_specs = (
        P("tmpl", "seg", None, None),
        P("tmpl", "seg"),
        P(("tmpl", "seg"), None),
        P(("tmpl", "seg"), None),
    )
    return jax.shard_map(shards, mesh=mesh, in_specs=in_specs, out_specs=out_specs, check_vma=False)
```

```python
import functools
import math

import jax
import jax.numpy as jnp
import numpy as np
import ml_dtypes
from jax import lax
from jax.experimental import pallas as pl
from jax.experimental.pallas import tpu as pltpu
from jax.sharding import PartitionSpec as P

BANDS = 16
ROWS = 512
COLS = 1024
BINS = ROWS * COLS
BLOCK = 32
SLOTS = 256
PAIRS = 128
F32 = jnp.float32
BF16 = jnp.bfloat16
VMEM = pl.BlockSpec(memory_space=pltpu.VMEM)
SMEM = pl.BlockSpec(memory_space=pltpu.SMEM)
LIMIT = 48 * 1024 * 1024


def unit(numerator, modulus):
    angle = 2.0 * math.pi * (np.asarray(numerator, np.int64) % modulus) / modulus
    return np.cos(angle), np.sin(angle)


def row_matrices():
    out = np.zeros((4, 4, 256, 256), np.float32)
    n = np.arange(128)
    for p in range(4):
        for j in range(4):
            c, s = unit((4 * n[None, :] + j) * (4 * n[:, None] + p), 4 * ROWS)
            out[p, j] = np.block([[c, -s], [s, c]])
    return out.astype(ml_dtypes.bfloat16)


def col_matrices():
    out = np.zeros((4, 512, 512), np.float32)
    n = np.arange(256)
    for p in range(4):
        c, s = unit(n[:, None] * (4 * n[None, :] + p), COLS)
        out[p] = np.block([[c, s], [-s, c]])
    return out.astype(ml_dtypes.bfloat16)


def twiddles():
    out = np.zeros((4, 2, 128, 256), np.float32)
    u = np.arange(128)
    for p in range(4):
        c, s = unit((4 * u[:, None] + p) * np.arange(256)[None, :], BINS)
        out[p, 0], out[p, 1] = c, s
    return out


def swap(x, *moves):
    pairs = []
    for z in range(4):
        for y in range(4):
            for k in range(4):
                for core in range(2):
                    axis, mask = moves[core]
                    to = {
                        "z": (z ^ mask, y, k, core),
                        "y": (z, y ^ mask, k, core),
                        "x": (z, y, k ^ mask, core),
                        "core": (z, y, k, core ^ mask),
                    }[axis]
                    number = lambda v: ((v[0] * 4 + v[1]) * 4 + v[2]) * 2 + v[3]
                    pairs.append((number((z, y, k, core)), number(to)))
    return lax.ppermute(x, ("tmpl", "seg"), pairs)


def distance(position, swapped):
    apart = position ^ (position >> 1)
    return jnp.where(swapped, (4 - apart) & 3, apart)


def pack_kernel(template_ref, pair_ref, time_ref, count_ref, out_ref):
    out_ref[0, :64] = template_ref[0]
    out_ref[0, 64:128] = template_ref[1]
    time = time_ref[...]
    row = lax.broadcasted_iota(jnp.int32, (1, SLOTS), 1)
    pair = jnp.where(row < count_ref[0], pair_ref[...], 255)
    line = jnp.concatenate([pair, time >> 16, (time >> 8) & 255, time & 255], axis=1)
    out_ref[0, 128:] = jnp.broadcast_to(line.astype(F32), (16, COLS)).astype(BF16)


def pack_lists(template, pairs, times, counts):
    return pl.pallas_call(
        pack_kernel,
        out_shape=jax.ShapeDtypeStruct((1, 144, COLS), BF16),
        in_specs=[VMEM, VMEM, VMEM, SMEM],
        out_specs=VMEM,
        cost_estimate=pl.CostEstimate(flops=100_000, bytes_accessed=600_000, transcendentals=0),
        name="pack_lists",
    )(template, pairs, times, counts)


def route_kernel(place, own_ref, other_ref, out_ref):
    z, y, x, core = place[0], place[1], place[2], place[3]
    seat = 2 * x + core
    row = lax.broadcasted_iota(jnp.int32, (16, SLOTS), 1).astype(F32)
    owner = (lax.broadcasted_iota(jnp.int32, (16, SLOTS), 0) * 8 + seat).astype(F32)
    lane = lax.broadcasted_iota(jnp.int32, (16, SLOTS), 1)
    out = jnp.zeros((16, SLOTS), F32)
    for turned, ref in enumerate((own_ref, other_ref)):
        holder = core ^ turned
        for position in range(4):
            line = ref[position, 128:144, :].astype(F32)[0:1]
            pair, high, mid, low = [line[:, 256 * k : 256 * k + 256] for k in range(4)]
            time = (high * 65536.0 + mid * 256.0 + low) + 1.0
            hit = pair == owner
            start = jnp.min(jnp.where(hit, row, 1e6), axis=1, keepdims=True)
            end = jnp.max(jnp.where(hit, row, -1.0), axis=1, keepdims=True)
            masks = (row == start, (row == end) & (end > start))
            source = 8 * (4 * z + y) + 2 * (x ^ distance(position, holder == 1)) + holder
            for slot, mask in enumerate(masks):
                value = jnp.sum(jnp.where(mask, time, 0.0), axis=1, keepdims=True)
                out = jnp.where(lane == PAIRS * slot + source, value, out)
    out_ref[...] = out.astype(jnp.int32)


def route_lists(place, own, other):
    return pl.pallas_call(
        route_kernel,
        out_shape=jax.ShapeDtypeStruct((16, SLOTS), jnp.int32),
        in_specs=[SMEM, VMEM, VMEM],
        out_specs=VMEM,
        compiler_params=pltpu.CompilerParams(vmem_limit_bytes=8 * 1024 * 1024),
        cost_estimate=pl.CostEstimate(flops=1_000_000, bytes_accessed=300_000, transcendentals=0),
        name="route_lists",
    )(place, own, other)


def order_kernel(place, own_ref, other_ref, out_ref, power_ref):
    x, core = place[2], place[3]
    for turned, ref in enumerate((own_ref, other_ref)):
        holder = core ^ turned

        def one(position, carry, ref=ref, holder=holder):
            rank = 2 * (x ^ distance(position, holder == 1)) + holder
            for half in range(2):
                total = jnp.zeros((8, 128), F32)
                for part in range(2):
                    rows = pl.ds(64 * part + 32 * half, 32)
                    h = ref[position, rows, :]
                    out_ref[part, pl.ds(pl.multiple_of(64 * rank + 32 * half, 32), 32), :] = h
                    h = h.astype(F32)
                    power = h * h
                    for r in range(0, 32, 8):
                        for c in range(0, COLS, 128):
                            total = total + power[r : r + 8, c : c + 128]
                whole = jnp.sum(total, axis=(0, 1), keepdims=True)
                power_ref[pl.ds(2 * rank + half, 1), :] = jnp.broadcast_to(whole, (1, SLOTS))
            return carry

        lax.fori_loop(0, 4, one, 0)


def order_template(place, own, other):
    return pl.pallas_call(
        order_kernel,
        out_shape=(
            jax.ShapeDtypeStruct((2, ROWS, COLS), BF16),
            jax.ShapeDtypeStruct((BANDS, SLOTS), F32),
        ),
        in_specs=[SMEM, VMEM, VMEM],
        out_specs=(VMEM, VMEM),
        compiler_params=pltpu.CompilerParams(vmem_limit_bytes=12 * 1024 * 1024),
        cost_estimate=pl.CostEstimate(flops=3_000_000, bytes_accessed=4_000_000, transcendentals=0),
        name="order_template",
    )(place, own, other)


def list_masks(pair_ref, count_ref):
    shape = (PAIRS, SLOTS)
    row = lax.broadcasted_iota(jnp.int32, shape, 1).astype(F32)
    owner = lax.broadcasted_iota(jnp.int32, shape, 0)
    hit = (pair_ref[...] == owner) & (row < count_ref[0].astype(F32))
    low = jnp.min(jnp.where(hit, row, 1e6), axis=1, keepdims=True)
    high = jnp.max(jnp.where(hit, row, -1.0), axis=1, keepdims=True)
    return hit & (row == low), hit & (row == high) & (high > low)


def take_kernel(pair_ref, count_ref, back_ref, chi_ref, snr_ref):
    first, second = list_masks(pair_ref, count_ref)
    for part, out_ref in enumerate((chi_ref, snr_ref)):
        one = jnp.where(first, back_ref[:, 2 * part : 2 * part + 1], 0.0)
        two = jnp.where(second, back_ref[:, 2 * part + 1 : 2 * part + 2], 0.0)
        out_ref[...] = jnp.sum(one + two, axis=0, keepdims=True)


def take_results(pairs, counts, back):
    return pl.pallas_call(
        take_kernel,
        out_shape=(jax.ShapeDtypeStruct((1, SLOTS), F32),) * 2,
        in_specs=[VMEM, SMEM, VMEM],
        out_specs=(VMEM, VMEM),
        cost_estimate=pl.CostEstimate(flops=500_000, bytes_accessed=70_000, transcendentals=0),
        name="take_results",
    )(pairs, counts, back)


def angle_parts(numerator, modulus):
    angles = (2.0 * math.pi / modulus) * (numerator & (modulus - 1)).astype(F32)
    return jnp.cos(angles), jnp.sin(angles)


def probe_kernel(list_ref, one_ref, two_ref, shift_ref, band_ref, time_ref):
    t = jnp.sum(list_ref[...].astype(F32), axis=0, keepdims=True).astype(jnp.int32) - 1
    time_ref[...] = t
    t = jnp.maximum(t, 0)
    step = lax.broadcasted_iota(jnp.int32, (32, SLOTS), 0)
    low_r, low_i = angle_parts(step * t, BINS)
    high_r, high_i = angle_parts(step * 32 * t, BINS)
    shift_ref[0], shift_ref[1] = angle_parts(step * t, ROWS)
    band_ref[0], band_ref[1] = angle_parts(step[:BANDS] * t, BANDS)
    for h in range(32):
        hr, hi = high_r[h : h + 1], high_i[h : h + 1]
        pr = (hr * low_r - hi * low_i).astype(BF16)
        pi = (hr * low_i + hi * low_r).astype(BF16)
        rows = pl.ds(32 * h, 32)
        one_ref[rows, :SLOTS] = pr
        one_ref[rows, SLOTS:] = pi
        two_ref[rows, :SLOTS] = -pi
        two_ref[rows, SLOTS:] = pr


def probes(lists):
    return pl.pallas_call(
        probe_kernel,
        out_shape=(
            jax.ShapeDtypeStruct((COLS, 2 * SLOTS), BF16),
            jax.ShapeDtypeStruct((COLS, 2 * SLOTS), BF16),
            jax.ShapeDtypeStruct((2, 32, SLOTS), F32),
            jax.ShapeDtypeStruct((2, BANDS, SLOTS), F32),
            jax.ShapeDtypeStruct((1, SLOTS), jnp.int32),
        ),
        in_specs=[VMEM],
        out_specs=(VMEM,) * 5,
        compiler_params=pltpu.CompilerParams(vmem_limit_bytes=LIMIT),
        cost_estimate=pl.CostEstimate(flops=4_000_000, bytes_accessed=2_200_000, transcendentals=60_000),
        name="probes",
    )(lists)


def block_place(place, det, late, early):
    z, y, core = place[0], place[1], place[3]
    late, early = distance(late, core == 1), distance(early, core == 1)
    return (z ^ late, y ^ early) if det == 0 else (z ^ early, y ^ late)


def spectra_kernel(half, place, template_ref, part0, part1, spec):
    for det, part in enumerate((part0, part1)):

        def one_block(m, carry, det=det, part=part):
            zz, yy = block_place(place, det, 2 * half + (m >> 2), m & 3)
            rows = pl.ds(pl.multiple_of(128 * zz + 32 * yy, 32), 32)
            for lane in range(0, COLS, 256):
                cols = pl.ds(lane, 256)
                hr = template_ref[0, rows, cols].astype(F32)
                hi = template_ref[1, rows, cols].astype(F32)
                xr = part[m, 0, :, cols].astype(F32)
                xi = part[m, 1, :, cols].astype(F32)
                spec[0, 8 * det + m, :, cols] = (hr * xr + hi * xi).astype(BF16)
                spec[1, 8 * det + m, :, cols] = (hr * xi - hi * xr).astype(BF16)
            return carry

        lax.fori_loop(0, 8, one_block, 0, unroll=2)


def spectra(half, place, template, parts):
    return pl.pallas_call(
        functools.partial(spectra_kernel, half),
        out_shape=jax.ShapeDtypeStruct((2, 16, 32, COLS), BF16),
        in_specs=[SMEM, VMEM, VMEM, VMEM],
        out_specs=VMEM,
        compiler_params=pltpu.CompilerParams(vmem_limit_bytes=12 * 1024 * 1024),
        cost_estimate=pl.CostEstimate(flops=3_000_000, bytes_accessed=6_000_000, transcendentals=0),
        name=("spectra_early", "spectra_late")[half],
    )(place, template, *parts)


def veto_kernel(place, power_ref, time_ref, one_ref, two_ref, shift_ref, band_ref, s0, s1, result_ref, sum_ref):
    sr, si = shift_ref[0], shift_ref[1]
    for half, spec in enumerate((s0, s1)):
        out = jnp.dot(spec[0].reshape(512, COLS), one_ref[...], preferred_element_type=F32)
        out = out + jnp.dot(spec[1].reshape(512, COLS), two_ref[...], preferred_element_type=F32)
        for det in range(2):
            for m in range(8):
                i = 8 * det + m
                yr = out[32 * i : 32 * i + 32, :SLOTS]
                yi = out[32 * i : 32 * i + 32, SLOTS:]
                ar = jnp.sum(yr * sr - yi * si, axis=0, keepdims=True)
                ai = jnp.sum(yr * si + yi * sr, axis=0, keepdims=True)
                zz, yy = block_place(place, det, 2 * half + (m >> 2), m & 3)
                band = 4 * zz + yy
                er = band_ref[0, pl.ds(band, 1), :]
                ei = band_ref[1, pl.ds(band, 1), :]
                sum_ref[pl.ds(BANDS * det + band, 1), :SLOTS] = ar * er - ai * ei
                sum_ref[pl.ds(BANDS * det + band, 1), SLOTS:] = ar * ei + ai * er
    power = power_ref[...]
    sigma = jnp.sum(power, axis=0, keepdims=True)
    weight = power / sigma
    chi = jnp.zeros((1, SLOTS), F32)
    snr = jnp.zeros((1, SLOTS), F32)
    for det in range(2):
        rows = pl.ds(BANDS * det, BANDS)
        br, bi = sum_ref[rows, :SLOTS], sum_ref[rows, SLOTS:]
        tr = jnp.sum(br, axis=0, keepdims=True)
        ti = jnp.sum(bi, axis=0, keepdims=True)
        dr = br - weight * tr
        di = bi - weight * ti
        chi = chi + jnp.sum((dr * dr + di * di) / (weight * sigma), axis=0, keepdims=True)
        snr = snr + (tr * tr + ti * ti)
    usable = time_ref[...] >= 0
    chi = jnp.where(usable, chi / (4.0 * (BANDS - 1)), 0.0)
    snr = jnp.where(usable, snr / (2.0 * sigma), 0.0)
    lines = [chi[:, :128], chi[:, 128:], snr[:, :128], snr[:, 128:], sigma[:, :128], jnp.zeros((123, 128), F32)]
    result_ref[...] = jnp.concatenate(lines, axis=0).T


def veto(place, power, times, tables, specs):
    return pl.pallas_call(
        veto_kernel,
        out_shape=jax.ShapeDtypeStruct((PAIRS, 128), F32),
        in_specs=[SMEM] + [VMEM] * 8,
        out_specs=VMEM,
        scratch_shapes=[pltpu.VMEM((2 * BANDS, 2 * SLOTS), F32)],
        compiler_params=pltpu.CompilerParams(vmem_limit_bytes=20 * 1024 * 1024),
        cost_estimate=pl.CostEstimate(
            flops=2_200_000_000, bytes_accessed=6_000_000, transcendentals=0
        ),
        name="veto",
    )(place, power, times, *tables, *specs)


def series_kernel(
    place, s0_hbm, s1_hbm, result_hbm, rows_hbm, turn_hbm, cols_hbm, out_hbm, peak_ref,
    s0, s1, sigma_ref, rows_ref, turn_ref, cols_ref, x_ref, g_ref, w_ref, v_ref, t_ref, o_ref, sems,
):
    copies = [
        pltpu.make_async_copy(src, dst, sems.at[k])
        for k, (src, dst) in enumerate(
            (
                (s0_hbm.at[:, :8], s0.at[:, :8]),
                (s1_hbm.at[:, :8], s1.at[:, :8]),
                (s0_hbm.at[:, 8:], s0.at[:, 8:]),
                (s1_hbm.at[:, 8:], s1.at[:, 8:]),
                *[
                    pair
                    for p in range(4)
                    for pair in (
                        (rows_hbm.at[p], rows_ref.at[p]),
                        (turn_hbm.at[p], turn_ref.at[p]),
                    )
                ],
                (cols_hbm, cols_ref),
                (result_hbm.at[:8], sigma_ref),
            )
        )
    ]
    for copy in copies:
        copy.start()
    specs = (s0, s1)
    z, y, core = place[0], place[1], place[3]

    def four(q):
        (r0, i0), (r1, i1), (r2, i2), (r3, i3) = q
        ar, ai = r0 + r2, i0 + i2
        br, bi = r1 + r3, i1 + i3
        cr, ci = r0 - r2, i0 - i2
        dr, di = r1 - r3, i1 - i3
        return (
            (ar + br, ai + bi),
            (cr - di, ci + dr),
            (ar - br, ai - bi),
            (cr + di, ci - dr),
        )

    turned = ((z & 1) ^ core) == 1

    def fold(det, yy, load):
        def chunk(k, carry):
            cols = pl.ds(pl.multiple_of(k * 256, 256), 256)
            q = [(load(o, 0, cols).astype(F32), load(o, 1, cols).astype(F32)) for o in (0, 1, 3, 2)]
            for p, (re, im) in enumerate(four(q)):
                to = jnp.where(turned, (4 - p) & 3, p)
                x_ref[det, to, pl.ds(pl.multiple_of(32 * yy, 32), 32), cols] = re.astype(BF16)
                x_ref[det, to, pl.ds(pl.multiple_of(128 + 32 * yy, 32), 32), cols] = im.astype(BF16)
            return carry

        lax.fori_loop(0, 4, chunk, 0)

    for det in range(2):
        copies[2 * det].wait()
        copies[2 * det + 1].wait()

        for m in range(4):
            if det == 0:
                load = lambda o, k, cols: specs[o >> 1][k, 4 * (o & 1) + m, :, cols]
            else:
                load = lambda o, k, cols: specs[m >> 1][k, 8 + 4 * (m & 1) + o, :, cols]
            fold(det, y ^ distance(m, core == 1), load)

    def first(step):
        p, det = divmod(step, 2)
        if det == 0:
            copies[4 + 2 * p].wait()
            copies[5 + 2 * p].wait()
        for j in range(4):
            cols = pl.ds(256 * j, 256)
            g_ref[step % 2, :, cols] = jnp.dot(
                rows_ref[p, j], x_ref[det, p, :, cols], preferred_element_type=F32
            )

    def turn(step):
        p, det = divmod(step, 2)
        for r in range(0, 128, 16):
            h = []
            for j in range(4):
                cols = pl.ds(256 * j, 256)
                h.append((g_ref[step % 2, pl.ds(r, 16), cols], g_ref[step % 2, pl.ds(128 + r, 16), cols]))
            tr = turn_ref[p, 0, pl.ds(r, 16), :]
            ti = turn_ref[p, 1, pl.ds(r, 16), :]
            rows = pl.ds(128 * p + r, 16)
            for k, (re, im) in enumerate(four(h)):
                w_ref[k, det, rows, :256] = (re * tr - im * ti).astype(BF16)
                w_ref[k, det, rows, 256:] = (re * ti + im * tr).astype(BF16)

    first(0)
    for step in range(8):
        if step < 7:
            first(step + 1)
        turn(step)
    copies[12].wait()
    copies[13].wait()

    scale = 1.0 / (2.0 * sigma_ref[0, 4])

    def second(k):
        for det in range(2):
            v_ref[k % 2, det] = jnp.dot(w_ref[k, det], cols_ref[k], preferred_element_type=F32)

    def power(k, best):
        for p in range(4):
            for r in range(0, 128, 16):
                rows = pl.ds(128 * p + r, 16)
                v = [
                    v_ref[k % 2, det, rows, pl.ds(256 * part, 256)]
                    for det in range(2)
                    for part in range(2)
                ]
                total = (v[0] * v[0] + v[1] * v[1] + v[2] * v[2] + v[3] * v[3]) * scale
                best = jnp.maximum(best, jnp.maximum(total[:8], total[8:]))
                for half in range(2):
                    t_ref[2 * k + half, pl.ds(4 * r + p, 16, stride=4), :] = total[
                        :, 128 * half : 128 * half + 128
                    ]
        return best

    best = jnp.zeros((8, 256), F32)
    second(0)
    for k in range(4):
        if k < 3:
            second(k + 1)
        best = power(k, best)
    peak_ref[...] = jnp.max(best, axis=(0, 1), keepdims=True)
    for i in range(4):
        for k in range(4):
            for half in range(2):
                tile = t_ref[2 * k + half, pl.ds(128 * i, 128), :]
                o_ref[i, pl.ds(512 * half + k, 128, stride=4), :] = tile.T
        copy = pltpu.make_async_copy(
            o_ref.at[i], out_hbm.at[:, pl.ds(128 * i, 128)], sems.at[14 + i]
        )
        copy.start()
        copies.append(copy)
    for copy in copies[14:]:
        copy.wait()


def series(place, specs, result, rows, turns, cols):
    hbm = pl.BlockSpec(memory_space=pltpu.HBM)
    return pl.pallas_call(
        series_kernel,
        out_shape=(
            jax.ShapeDtypeStruct((COLS, ROWS), F32),
            jax.ShapeDtypeStruct((1, 1), F32),
        ),
        in_specs=[SMEM] + [hbm] * 6,
        out_specs=(hbm, VMEM),
        scratch_shapes=[
            pltpu.VMEM(specs[0].shape, BF16),
            pltpu.VMEM(specs[1].shape, BF16),
            pltpu.VMEM((8, 128), F32),
            pltpu.VMEM(rows.shape, rows.dtype),
            pltpu.VMEM(turns.shape, turns.dtype),
            pltpu.VMEM(cols.shape, cols.dtype),
            pltpu.VMEM((2, 4, 256, COLS), BF16),
            pltpu.VMEM((2, 256, COLS), F32),
            pltpu.VMEM((4, 2, ROWS, 512), BF16),
            pltpu.VMEM((2, 2, ROWS, 512), F32),
            pltpu.VMEM((8, ROWS, 128), F32),
            pltpu.VMEM((4, COLS, 128), F32),
            pltpu.SemaphoreType.DMA((18,)),
        ],
        compiler_params=pltpu.CompilerParams(vmem_limit_bytes=60 * 1024 * 1024),
        cost_estimate=pl.CostEstimate(
            flops=3_300_000_000, bytes_accessed=13_000_000, transcendentals=0
        ),
        name="series",
    )(place, *specs, result, rows, turns, cols)


def shards(strain, templates, trig_pair, trig_time, trig_counts):
    device = lax.axis_index("tmpl")
    seat = lax.axis_index("seg")
    place = jnp.stack([device // 4, device % 4, seat // 2, seat % 2]).astype(jnp.int32)

    a, b = strain[:, 0, 0][None], strain[:, 1, 0][None]
    t = pack_lists(templates[:, 0], trig_pair, trig_time, trig_counts)
    for step, (near, far) in enumerate(((1, 3), (3, 1), (1, 3), (3, 1))):
        more_a = swap(a, ("yyzz"[step], near), ("yyzz"[step], far))
        more_b = swap(b, ("zzyy"[step], near), ("zzyy"[step], far))
        if step < 2:
            t = jnp.concatenate([t, swap(t, ("x", near), ("x", far))])
        if step < 3:
            a, b = jnp.concatenate([a, more_a]), jnp.concatenate([b, more_b])
    other_t = swap(t, ("core", 1), ("core", 1))

    outgoing = route_lists(place, t, other_t)
    incoming = lax.all_to_all(outgoing, "tmpl", split_axis=0, concat_axis=0, tiled=True)
    template, power = order_template(place, t, other_t)
    more_a, more_b, incoming = lax.optimization_barrier((more_a, more_b, incoming))
    specs = spectra(0, place, template, (a, b)), spectra(1, place, template, (more_a, more_b))
    *tables, times = probes(incoming)
    result = veto(place, power, times, tables, specs)
    back = lax.all_to_all(result, ("tmpl", "seg"), split_axis=0, concat_axis=0, tiled=True)
    snr_series, peak = series(
        place,
        specs,
        result,
        jnp.asarray(row_matrices()),
        jnp.asarray(twiddles()),
        jnp.asarray(col_matrices()),
    )
    chi, snr = take_results(trig_pair, trig_counts, back)
    return (snr_series[None, None], peak, chi, snr)


def solution(mesh):
    in_specs = (
        P(None, None, "seg", "tmpl", None),
        P(None, "tmpl", "seg", None),
        P(("tmpl", "seg"), None),
        P(("tmpl", "seg"), None),
        P(("tmpl", "seg")),
    )
    out_specs = (
        P("tmpl", "seg", None, None),
        P("tmpl", "seg"),
        P(("tmpl", "seg"), None),
        P(("tmpl", "seg"), None),
    )
    return jax.shard_map(shards, mesh=mesh, in_specs=in_specs, out_specs=out_specs, check_vma=False)
```

```python
import functools
import math

import jax
import jax.numpy as jnp
import numpy as np
import ml_dtypes
from jax import lax
from jax.experimental import pallas as pl
from jax.experimental.pallas import tpu as pltpu
from jax.sharding import PartitionSpec as P

BANDS = 16
ROWS = 512
COLS = 1024
BINS = ROWS * COLS
BLOCK = 32
SLOTS = 256
PAIRS = 128
F32 = jnp.float32
BF16 = jnp.bfloat16
VMEM = pl.BlockSpec(memory_space=pltpu.VMEM)
SMEM = pl.BlockSpec(memory_space=pltpu.SMEM)
LIMIT = 48 * 1024 * 1024


def unit(numerator, modulus):
    angle = 2.0 * math.pi * (np.asarray(numerator, np.int64) % modulus) / modulus
    return np.cos(angle), np.sin(angle)


def row_matrices():
    out = np.zeros((4, 4, 256, 256), np.float32)
    n = np.arange(128)
    for p in range(4):
        for j in range(4):
            c, s = unit((4 * n[None, :] + j) * (4 * n[:, None] + p), 4 * ROWS)
            out[p, j] = np.block([[c, -s], [s, c]])
    return out.astype(ml_dtypes.bfloat16)


def col_matrices():
    out = np.zeros((4, 512, 512), np.float32)
    n = np.arange(256)
    for p in range(4):
        c, s = unit(n[:, None] * (4 * n[None, :] + p), COLS)
        out[p] = np.block([[c, s], [-s, c]])
    return out.astype(ml_dtypes.bfloat16)


def twiddles():
    out = np.zeros((4, 2, 128, 256), np.float32)
    u = np.arange(128)
    for p in range(4):
        c, s = unit((4 * u[:, None] + p) * np.arange(256)[None, :], BINS)
        out[p, 0], out[p, 1] = c, s
    return out


def swap(x, *moves):
    pairs = []
    for z in range(4):
        for y in range(4):
            for k in range(4):
                for core in range(2):
                    axis, mask = moves[core]
                    to = {
                        "z": (z ^ mask, y, k, core),
                        "y": (z, y ^ mask, k, core),
                        "x": (z, y, k ^ mask, core),
                        "core": (z, y, k, core ^ mask),
                    }[axis]
                    number = lambda v: ((v[0] * 4 + v[1]) * 4 + v[2]) * 2 + v[3]
                    pairs.append((number((z, y, k, core)), number(to)))
    return lax.ppermute(x, ("tmpl", "seg"), pairs)


def distance(position, swapped):
    apart = position ^ (position >> 1)
    return jnp.where(swapped, (4 - apart) & 3, apart)


def pack_kernel(strain_ref, template_ref, pair_ref, time_ref, count_ref, a_ref, b_ref, out_ref):
    for part in range(2):
        a_ref[0, part] = strain_ref[part, 0, 0]
        b_ref[0, part] = strain_ref[part, 1, 0]
    out_ref[0, :64] = template_ref[0]
    out_ref[0, 64:128] = template_ref[1]
    time = time_ref[...]
    row = lax.broadcasted_iota(jnp.int32, (1, SLOTS), 1)
    pair = jnp.where(row < count_ref[0], pair_ref[...], 255)
    line = jnp.concatenate([pair, time >> 16, (time >> 8) & 255, time & 255], axis=1)
    out_ref[0, 128:] = jnp.broadcast_to(line.astype(F32), (16, COLS)).astype(BF16)


def pack_lists(strain, template, pairs, times, counts):
    return pl.pallas_call(
        pack_kernel,
        out_shape=(
            jax.ShapeDtypeStruct((1, 2, 32, COLS), BF16),
            jax.ShapeDtypeStruct((1, 2, 32, COLS), BF16),
            jax.ShapeDtypeStruct((1, 144, COLS), BF16),
        ),
        in_specs=[VMEM, VMEM, VMEM, VMEM, SMEM],
        out_specs=(VMEM,) * 3,
        cost_estimate=pl.CostEstimate(flops=100_000, bytes_accessed=600_000, transcendentals=0),
        name="pack_lists",
    )(strain, template, pairs, times, counts)


def route_kernel(place, own_ref, other_ref, out_ref):
    z, y, x, core = place[0], place[1], place[2], place[3]
    seat = 2 * x + core
    row = lax.broadcasted_iota(jnp.int32, (16, SLOTS), 1).astype(F32)
    owner = (lax.broadcasted_iota(jnp.int32, (16, SLOTS), 0) * 8 + seat).astype(F32)
    lane = lax.broadcasted_iota(jnp.int32, (16, SLOTS), 1)
    out = jnp.zeros((16, SLOTS), F32)
    for turned, ref in enumerate((own_ref, other_ref)):
        holder = core ^ turned
        for position in range(4):
            line = ref[position, 128:144, :].astype(F32)[0:1]
            pair, high, mid, low = [line[:, 256 * k : 256 * k + 256] for k in range(4)]
            time = (high * 65536.0 + mid * 256.0 + low) + 1.0
            hit = pair == owner
            start = jnp.min(jnp.where(hit, row, 1e6), axis=1, keepdims=True)
            end = jnp.max(jnp.where(hit, row, -1.0), axis=1, keepdims=True)
            masks = (row == start, (row == end) & (end > start))
            source = 8 * (4 * z + y) + 2 * (x ^ distance(position, holder == 1)) + holder
            for slot, mask in enumerate(masks):
                value = jnp.sum(jnp.where(mask, time, 0.0), axis=1, keepdims=True)
                out = jnp.where(lane == PAIRS * slot + source, value, out)
    out_ref[...] = out.astype(jnp.int32)


def route_lists(place, own, other):
    return pl.pallas_call(
        route_kernel,
        out_shape=jax.ShapeDtypeStruct((16, SLOTS), jnp.int32),
        in_specs=[SMEM, VMEM, VMEM],
        out_specs=VMEM,
        compiler_params=pltpu.CompilerParams(vmem_limit_bytes=8 * 1024 * 1024),
        cost_estimate=pl.CostEstimate(flops=1_000_000, bytes_accessed=300_000, transcendentals=0),
        name="route_lists",
    )(place, own, other)


def order_kernel(place, own_ref, other_ref, out_ref, power_ref):
    x, core = place[2], place[3]
    for turned, ref in enumerate((own_ref, other_ref)):
        holder = core ^ turned

        def one(position, carry, ref=ref, holder=holder):
            rank = 2 * (x ^ distance(position, holder == 1)) + holder
            for half in range(2):
                total = jnp.zeros((8, 128), F32)
                for part in range(2):
                    rows = pl.ds(64 * part + 32 * half, 32)
                    h = ref[position, rows, :]
                    out_ref[part, pl.ds(pl.multiple_of(64 * rank + 32 * half, 32), 32), :] = h
                    h = h.astype(F32)
                    power = h * h
                    for r in range(0, 32, 8):
                        for c in range(0, COLS, 128):
                            total = total + power[r : r + 8, c : c + 128]
                whole = jnp.sum(total, axis=(0, 1), keepdims=True)
                power_ref[pl.ds(2 * rank + half, 1), :] = jnp.broadcast_to(whole, (1, SLOTS))
            return carry

        lax.fori_loop(0, 4, one, 0)


def order_template(place, own, other):
    return pl.pallas_call(
        order_kernel,
        out_shape=(
            jax.ShapeDtypeStruct((2, ROWS, COLS), BF16),
            jax.ShapeDtypeStruct((BANDS, SLOTS), F32),
        ),
        in_specs=[SMEM, VMEM, VMEM],
        out_specs=(VMEM, VMEM),
        compiler_params=pltpu.CompilerParams(vmem_limit_bytes=12 * 1024 * 1024),
        cost_estimate=pl.CostEstimate(flops=3_000_000, bytes_accessed=4_000_000, transcendentals=0),
        name="order_template",
    )(place, own, other)


def list_masks(pair_ref, count_ref):
    shape = (PAIRS, SLOTS)
    row = lax.broadcasted_iota(jnp.int32, shape, 1).astype(F32)
    owner = lax.broadcasted_iota(jnp.int32, shape, 0)
    hit = (pair_ref[...] == owner) & (row < count_ref[0].astype(F32))
    low = jnp.min(jnp.where(hit, row, 1e6), axis=1, keepdims=True)
    high = jnp.max(jnp.where(hit, row, -1.0), axis=1, keepdims=True)
    return hit & (row == low), hit & (row == high) & (high > low)


def take_kernel(pair_ref, count_ref, back_ref, chi_ref, snr_ref):
    first, second = list_masks(pair_ref, count_ref)
    for part, out_ref in enumerate((chi_ref, snr_ref)):
        one = jnp.where(first, back_ref[:, 2 * part : 2 * part + 1], 0.0)
        two = jnp.where(second, back_ref[:, 2 * part + 1 : 2 * part + 2], 0.0)
        out_ref[...] = jnp.sum(one + two, axis=0, keepdims=True)


def take_results(pairs, counts, back):
    return pl.pallas_call(
        take_kernel,
        out_shape=(jax.ShapeDtypeStruct((1, SLOTS), F32),) * 2,
        in_specs=[VMEM, SMEM, VMEM],
        out_specs=(VMEM, VMEM),
        cost_estimate=pl.CostEstimate(flops=500_000, bytes_accessed=70_000, transcendentals=0),
        name="take_results",
    )(pairs, counts, back)


def angle_parts(numerator, modulus):
    angles = (2.0 * math.pi / modulus) * (numerator & (modulus - 1)).astype(F32)
    return jnp.cos(angles), jnp.sin(angles)


def probe_kernel(list_ref, one_ref, two_ref, shift_ref, band_ref, time_ref):
    t = jnp.sum(list_ref[...].astype(F32), axis=0, keepdims=True).astype(jnp.int32) - 1
    time_ref[...] = t
    t = jnp.maximum(t, 0)
    step = lax.broadcasted_iota(jnp.int32, (32, SLOTS), 0)
    low_r, low_i = angle_parts(step * t, BINS)
    high_r, high_i = angle_parts(step * 32 * t, BINS)
    shift_ref[0], shift_ref[1] = angle_parts(step * t, ROWS)
    band_ref[0], band_ref[1] = angle_parts(step[:BANDS] * t, BANDS)
    for h in range(32):
        hr, hi = high_r[h : h + 1], high_i[h : h + 1]
        pr = (hr * low_r - hi * low_i).astype(BF16)
        pi = (hr * low_i + hi * low_r).astype(BF16)
        rows = pl.ds(32 * h, 32)
        one_ref[rows, :SLOTS] = pr
        one_ref[rows, SLOTS:] = pi
        two_ref[rows, :SLOTS] = -pi
        two_ref[rows, SLOTS:] = pr


def probes(lists):
    return pl.pallas_call(
        probe_kernel,
        out_shape=(
            jax.ShapeDtypeStruct((COLS, 2 * SLOTS), BF16),
            jax.ShapeDtypeStruct((COLS, 2 * SLOTS), BF16),
            jax.ShapeDtypeStruct((2, 32, SLOTS), F32),
            jax.ShapeDtypeStruct((2, BANDS, SLOTS), F32),
            jax.ShapeDtypeStruct((1, SLOTS), jnp.int32),
        ),
        in_specs=[VMEM],
        out_specs=(VMEM,) * 5,
        compiler_params=pltpu.CompilerParams(vmem_limit_bytes=LIMIT),
        cost_estimate=pl.CostEstimate(flops=4_000_000, bytes_accessed=2_200_000, transcendentals=60_000),
        name="probes",
    )(lists)


def block_place(place, det, late, early):
    z, y, core = place[0], place[1], place[3]
    late, early = distance(late, core == 1), distance(early, core == 1)
    return (z ^ late, y ^ early) if det == 0 else (z ^ early, y ^ late)


def spectra_kernel(half, place, template_ref, part0, part1, spec):
    for det, part in enumerate((part0, part1)):

        def one_block(m, carry, det=det, part=part):
            zz, yy = block_place(place, det, 2 * half + (m >> 2), m & 3)
            rows = pl.ds(pl.multiple_of(128 * zz + 32 * yy, 32), 32)
            for lane in range(0, COLS, 256):
                cols = pl.ds(lane, 256)
                hr = template_ref[0, rows, cols].astype(F32)
                hi = template_ref[1, rows, cols].astype(F32)
                xr = part[m, 0, :, cols].astype(F32)
                xi = part[m, 1, :, cols].astype(F32)
                spec[0, 8 * det + m, :, cols] = (hr * xr + hi * xi).astype(BF16)
                spec[1, 8 * det + m, :, cols] = (hr * xi - hi * xr).astype(BF16)
            return carry

        lax.fori_loop(0, 8, one_block, 0, unroll=2)


def spectra(half, place, template, parts):
    return pl.pallas_call(
        functools.partial(spectra_kernel, half),
        out_shape=jax.ShapeDtypeStruct((2, 16, 32, COLS), BF16),
        in_specs=[SMEM, VMEM, VMEM, VMEM],
        out_specs=VMEM,
        compiler_params=pltpu.CompilerParams(vmem_limit_bytes=12 * 1024 * 1024),
        cost_estimate=pl.CostEstimate(flops=3_000_000, bytes_accessed=6_000_000, transcendentals=0),
        name=("spectra_early", "spectra_late")[half],
    )(place, template, *parts)


def veto_kernel(place, power_ref, time_ref, one_ref, two_ref, shift_ref, band_ref, s0, s1, result_ref, sum_ref):
    sr, si = shift_ref[0], shift_ref[1]
    for half, spec in enumerate((s0, s1)):
        out = jnp.dot(spec[0].reshape(512, COLS), one_ref[...], preferred_element_type=F32)
        out = out + jnp.dot(spec[1].reshape(512, COLS), two_ref[...], preferred_element_type=F32)
        for det in range(2):
            for m in range(8):
                i = 8 * det + m
                yr = out[32 * i : 32 * i + 32, :SLOTS]
                yi = out[32 * i : 32 * i + 32, SLOTS:]
                ar = jnp.sum(yr * sr - yi * si, axis=0, keepdims=True)
                ai = jnp.sum(yr * si + yi * sr, axis=0, keepdims=True)
                zz, yy = block_place(place, det, 2 * half + (m >> 2), m & 3)
                band = 4 * zz + yy
                er = band_ref[0, pl.ds(band, 1), :]
                ei = band_ref[1, pl.ds(band, 1), :]
                sum_ref[pl.ds(BANDS * det + band, 1), :SLOTS] = ar * er - ai * ei
                sum_ref[pl.ds(BANDS * det + band, 1), SLOTS:] = ar * ei + ai * er
    power = power_ref[...]
    sigma = jnp.sum(power, axis=0, keepdims=True)
    weight = power / sigma
    chi = jnp.zeros((1, SLOTS), F32)
    snr = jnp.zeros((1, SLOTS), F32)
    for det in range(2):
        rows = pl.ds(BANDS * det, BANDS)
        br, bi = sum_ref[rows, :SLOTS], sum_ref[rows, SLOTS:]
        tr = jnp.sum(br, axis=0, keepdims=True)
        ti = jnp.sum(bi, axis=0, keepdims=True)
        dr = br - weight * tr
        di = bi - weight * ti
        chi = chi + jnp.sum((dr * dr + di * di) / (weight * sigma), axis=0, keepdims=True)
        snr = snr + (tr * tr + ti * ti)
    usable = time_ref[...] >= 0
    chi = jnp.where(usable, chi / (4.0 * (BANDS - 1)), 0.0)
    snr = jnp.where(usable, snr / (2.0 * sigma), 0.0)
    lines = [chi[:, :128], chi[:, 128:], snr[:, :128], snr[:, 128:], sigma[:, :128], jnp.zeros((123, 128), F32)]
    result_ref[...] = jnp.concatenate(lines, axis=0).T


def veto(place, power, times, tables, specs):
    return pl.pallas_call(
        veto_kernel,
        out_shape=jax.ShapeDtypeStruct((PAIRS, 128), F32),
        in_specs=[SMEM] + [VMEM] * 8,
        out_specs=VMEM,
        scratch_shapes=[pltpu.VMEM((2 * BANDS, 2 * SLOTS), F32)],
        compiler_params=pltpu.CompilerParams(vmem_limit_bytes=20 * 1024 * 1024),
        cost_estimate=pl.CostEstimate(
            flops=2_200_000_000, bytes_accessed=6_000_000, transcendentals=0
        ),
        name="veto",
    )(place, power, times, *tables, *specs)


def series_kernel(
    place, s0_hbm, s1_hbm, result_hbm, rows_hbm, turn_hbm, cols_hbm, out_hbm, peak_ref,
    s0, s1, sigma_ref, rows_ref, turn_ref, cols_ref, x_ref, g_ref, w_ref, v_ref, t_ref, o_ref, sems,
):
    copies = [
        pltpu.make_async_copy(src, dst, sems.at[k])
        for k, (src, dst) in enumerate(
            (
                (s0_hbm.at[:, :8], s0.at[:, :8]),
                (s1_hbm.at[:, :8], s1.at[:, :8]),
                (s0_hbm.at[:, 8:], s0.at[:, 8:]),
                (s1_hbm.at[:, 8:], s1.at[:, 8:]),
                *[
                    pair
                    for p in range(4)
                    for pair in (
                        (rows_hbm.at[p], rows_ref.at[p]),
                        (turn_hbm.at[p], turn_ref.at[p]),
                    )
                ],
                (cols_hbm, cols_ref),
                (result_hbm.at[:8], sigma_ref),
            )
        )
    ]
    for copy in copies:
        copy.start()
    specs = (s0, s1)
    z, y, core = place[0], place[1], place[3]

    def four(q):
        (r0, i0), (r1, i1), (r2, i2), (r3, i3) = q
        ar, ai = r0 + r2, i0 + i2
        br, bi = r1 + r3, i1 + i3
        cr, ci = r0 - r2, i0 - i2
        dr, di = r1 - r3, i1 - i3
        return (
            (ar + br, ai + bi),
            (cr - di, ci + dr),
            (ar - br, ai - bi),
            (cr + di, ci - dr),
        )

    turned = ((z & 1) ^ core) == 1

    def fold(det, yy, load):
        def chunk(k, carry):
            cols = pl.ds(pl.multiple_of(k * 256, 256), 256)
            q = [(load(o, 0, cols).astype(F32), load(o, 1, cols).astype(F32)) for o in (0, 1, 3, 2)]
            for p, (re, im) in enumerate(four(q)):
                to = jnp.where(turned, (4 - p) & 3, p)
                x_ref[det, to, pl.ds(pl.multiple_of(32 * yy, 32), 32), cols] = re.astype(BF16)
                x_ref[det, to, pl.ds(pl.multiple_of(128 + 32 * yy, 32), 32), cols] = im.astype(BF16)
            return carry

        lax.fori_loop(0, 4, chunk, 0)

    for det in range(2):
        copies[2 * det].wait()
        copies[2 * det + 1].wait()

        for m in range(4):
            if det == 0:
                load = lambda o, k, cols: specs[o >> 1][k, 4 * (o & 1) + m, :, cols]
            else:
                load = lambda o, k, cols: specs[m >> 1][k, 8 + 4 * (m & 1) + o, :, cols]
            fold(det, y ^ distance(m, core == 1), load)

    def first(step):
        p, det = divmod(step, 2)
        if det == 0:
            copies[4 + 2 * p].wait()
            copies[5 + 2 * p].wait()
        for j in range(4):
            cols = pl.ds(256 * j, 256)
            g_ref[step % 2, :, cols] = jnp.dot(
                rows_ref[p, j], x_ref[det, p, :, cols], preferred_element_type=F32
            )

    def turn(step):
        p, det = divmod(step, 2)
        for r in range(0, 128, 16):
            h = []
            for j in range(4):
                cols = pl.ds(256 * j, 256)
                h.append((g_ref[step % 2, pl.ds(r, 16), cols], g_ref[step % 2, pl.ds(128 + r, 16), cols]))
            tr = turn_ref[p, 0, pl.ds(r, 16), :]
            ti = turn_ref[p, 1, pl.ds(r, 16), :]
            rows = pl.ds(128 * p + r, 16)
            for k, (re, im) in enumerate(four(h)):
                w_ref[k, det, rows, :256] = (re * tr - im * ti).astype(BF16)
                w_ref[k, det, rows, 256:] = (re * ti + im * tr).astype(BF16)

    first(0)
    for step in range(8):
        if step < 7:
            first(step + 1)
        turn(step)
    copies[12].wait()
    copies[13].wait()

    scale = 1.0 / (2.0 * sigma_ref[0, 4])

    def second(k):
        for det in range(2):
            v_ref[k % 2, det] = jnp.dot(w_ref[k, det], cols_ref[k], preferred_element_type=F32)

    def power(k, best):
        for p in range(4):
            for r in range(0, 128, 16):
                rows = pl.ds(128 * p + r, 16)
                v = [
                    v_ref[k % 2, det, rows, pl.ds(256 * part, 256)]
                    for det in range(2)
                    for part in range(2)
                ]
                total = (v[0] * v[0] + v[1] * v[1] + v[2] * v[2] + v[3] * v[3]) * scale
                best = jnp.maximum(best, jnp.maximum(total[:8], total[8:]))
                for half in range(2):
                    t_ref[2 * k + half, pl.ds(4 * r + p, 16, stride=4), :] = total[
                        :, 128 * half : 128 * half + 128
                    ]
        return best

    best = jnp.zeros((8, 256), F32)
    second(0)
    for k in range(4):
        if k < 3:
            second(k + 1)
        best = power(k, best)
    peak_ref[...] = jnp.max(best, axis=(0, 1), keepdims=True)
    for i in range(4):
        for k in range(4):
            for half in range(2):
                tile = t_ref[2 * k + half, pl.ds(128 * i, 128), :]
                o_ref[i, pl.ds(512 * half + k, 128, stride=4), :] = tile.T
        copy = pltpu.make_async_copy(
            o_ref.at[i], out_hbm.at[:, pl.ds(128 * i, 128)], sems.at[14 + i]
        )
        copy.start()
        copies.append(copy)
    for copy in copies[14:]:
        copy.wait()


def series(place, specs, result, rows, turns, cols):
    hbm = pl.BlockSpec(memory_space=pltpu.HBM)
    return pl.pallas_call(
        series_kernel,
        out_shape=(
            jax.ShapeDtypeStruct((COLS, ROWS), F32),
            jax.ShapeDtypeStruct((1, 1), F32),
        ),
        in_specs=[SMEM] + [hbm] * 6,
        out_specs=(hbm, VMEM),
        scratch_shapes=[
            pltpu.VMEM(specs[0].shape, BF16),
            pltpu.VMEM(specs[1].shape, BF16),
            pltpu.VMEM((8, 128), F32),
            pltpu.VMEM(rows.shape, rows.dtype),
            pltpu.VMEM(turns.shape, turns.dtype),
            pltpu.VMEM(cols.shape, cols.dtype),
            pltpu.VMEM((2, 4, 256, COLS), BF16),
            pltpu.VMEM((2, 256, COLS), F32),
            pltpu.VMEM((4, 2, ROWS, 512), BF16),
            pltpu.VMEM((2, 2, ROWS, 512), F32),
            pltpu.VMEM((8, ROWS, 128), F32),
            pltpu.VMEM((4, COLS, 128), F32),
            pltpu.SemaphoreType.DMA((18,)),
        ],
        compiler_params=pltpu.CompilerParams(vmem_limit_bytes=60 * 1024 * 1024),
        cost_estimate=pl.CostEstimate(
            flops=3_300_000_000, bytes_accessed=13_000_000, transcendentals=0
        ),
        name="series",
    )(place, *specs, result, rows, turns, cols)


def shards(strain, templates, trig_pair, trig_time, trig_counts):
    device = lax.axis_index("tmpl")
    seat = lax.axis_index("seg")
    place = jnp.stack([device // 4, device % 4, seat // 2, seat % 2]).astype(jnp.int32)

    a, b, t = pack_lists(strain, templates[:, 0], trig_pair, trig_time, trig_counts)
    for step, (near, far) in enumerate(((1, 3), (3, 1), (1, 3), (3, 1))):
        more_a = swap(a, ("yyzz"[step], near), ("yyzz"[step], far))
        more_b = swap(b, ("zzyy"[step], near), ("zzyy"[step], far))
        if step < 2:
            t = jnp.concatenate([t, swap(t, ("x", near), ("x", far))])
        if step < 3:
            a, b = jnp.concatenate([a, more_a]), jnp.concatenate([b, more_b])
    other_t = swap(t, ("core", 1), ("core", 1))

    outgoing = route_lists(place, t, other_t)
    incoming = lax.all_to_all(outgoing, "tmpl", split_axis=0, concat_axis=0, tiled=True)
    template, power = order_template(place, t, other_t)
    more_a, more_b, incoming = lax.optimization_barrier((more_a, more_b, incoming))
    specs = spectra(0, place, template, (a, b)), spectra(1, place, template, (more_a, more_b))
    *tables, times = probes(incoming)
    result = veto(place, power, times, tables, specs)
    back = lax.all_to_all(result, ("tmpl", "seg"), split_axis=0, concat_axis=0, tiled=True)
    snr_series, peak = series(
        place,
        specs,
        result,
        jnp.asarray(row_matrices()),
        jnp.asarray(twiddles()),
        jnp.asarray(col_matrices()),
    )
    chi, snr = take_results(trig_pair, trig_counts, back)
    return (snr_series[None, None], peak, chi, snr)


def solution(mesh):
    in_specs = (
        P(None, None, "seg", "tmpl", None),
        P(None, "tmpl", "seg", None),
        P(("tmpl", "seg"), None),
        P(("tmpl", "seg"), None),
        P(("tmpl", "seg")),
    )
    out_specs = (
        P("tmpl", "seg", None, None),
        P("tmpl", "seg"),
        P(("tmpl", "seg"), None),
        P(("tmpl", "seg"), None),
    )
    return jax.shard_map(shards, mesh=mesh, in_specs=in_specs, out_specs=out_specs, check_vma=False)
```

```python
import functools
import math

import jax
import jax.numpy as jnp
import numpy as np
import ml_dtypes
from jax import lax
from jax.experimental import pallas as pl
from jax.experimental.pallas import tpu as pltpu
from jax.sharding import PartitionSpec as P

BANDS = 16
ROWS = 512
COLS = 1024
BINS = ROWS * COLS
BLOCK = 32
SLOTS = 256
PAIRS = 128
F32 = jnp.float32
BF16 = jnp.bfloat16
VMEM = pl.BlockSpec(memory_space=pltpu.VMEM)
SMEM = pl.BlockSpec(memory_space=pltpu.SMEM)
LIMIT = 48 * 1024 * 1024


def unit(numerator, modulus):
    angle = 2.0 * math.pi * (np.asarray(numerator, np.int64) % modulus) / modulus
    return np.cos(angle), np.sin(angle)


def row_matrices():
    out = np.zeros((4, 4, 256, 256), np.float32)
    n = np.arange(128)
    for p in range(4):
        for j in range(4):
            c, s = unit((4 * n[None, :] + j) * (4 * n[:, None] + p), 4 * ROWS)
            out[p, j] = np.block([[c, -s], [s, c]])
    return out.astype(ml_dtypes.bfloat16)


def col_matrices():
    out = np.zeros((4, 512, 512), np.float32)
    n = np.arange(256)
    for p in range(4):
        c, s = unit(n[:, None] * (4 * n[None, :] + p), COLS)
        out[p] = np.block([[c, s], [-s, c]])
    return out.astype(ml_dtypes.bfloat16)


def twiddles():
    out = np.zeros((4, 2, 128, 256), np.float32)
    u = np.arange(128)
    for p in range(4):
        c, s = unit((4 * u[:, None] + p) * np.arange(256)[None, :], BINS)
        out[p, 0], out[p, 1] = c, s
    return out


def swap(x, *moves):
    pairs = []
    for z in range(4):
        for y in range(4):
            for k in range(4):
                for core in range(2):
                    axis, mask = moves[core]
                    to = {
                        "z": (z ^ mask, y, k, core),
                        "y": (z, y ^ mask, k, core),
                        "x": (z, y, k ^ mask, core),
                        "core": (z, y, k, core ^ mask),
                    }[axis]
                    number = lambda v: ((v[0] * 4 + v[1]) * 4 + v[2]) * 2 + v[3]
                    pairs.append((number((z, y, k, core)), number(to)))
    return lax.ppermute(x, ("tmpl", "seg"), pairs)


def distance(position, swapped):
    apart = position ^ (position >> 1)
    return jnp.where(swapped, (4 - apart) & 3, apart)


def pack_kernel(strain_ref, template_ref, pair_ref, time_ref, count_ref, a_ref, b_ref, out_ref):
    for part in range(2):
        a_ref[0, part] = strain_ref[part, 0, 0]
        b_ref[0, part] = strain_ref[part, 1, 0]
    out_ref[0, :64] = template_ref[0]
    out_ref[0, 64:128] = template_ref[1]
    time = time_ref[...]
    row = lax.broadcasted_iota(jnp.int32, (1, SLOTS), 1)
    pair = jnp.where(row < count_ref[0], pair_ref[...], 255)
    line = jnp.concatenate([pair, time >> 16, (time >> 8) & 255, time & 255], axis=1)
    out_ref[0, 128:] = jnp.broadcast_to(line.astype(F32), (16, COLS)).astype(BF16)


def pack_lists(strain, template, pairs, times, counts):
    return pl.pallas_call(
        pack_kernel,
        out_shape=(
            jax.ShapeDtypeStruct((1, 2, 32, COLS), BF16),
            jax.ShapeDtypeStruct((1, 2, 32, COLS), BF16),
            jax.ShapeDtypeStruct((1, 144, COLS), BF16),
        ),
        in_specs=[VMEM, VMEM, VMEM, VMEM, SMEM],
        out_specs=(VMEM,) * 3,
        cost_estimate=pl.CostEstimate(flops=100_000, bytes_accessed=600_000, transcendentals=0),
        name="pack_lists",
    )(strain, template, pairs, times, counts)


def route_kernel(place, own_ref, other_ref, out_ref):
    z, y, x, core = place[0], place[1], place[2], place[3]
    seat = 2 * x + core
    row = lax.broadcasted_iota(jnp.int32, (16, SLOTS), 1).astype(F32)
    owner = (lax.broadcasted_iota(jnp.int32, (16, SLOTS), 0) * 8 + seat).astype(F32)
    lane = lax.broadcasted_iota(jnp.int32, (16, SLOTS), 1)
    out = jnp.zeros((16, SLOTS), F32)
    for turned, ref in enumerate((own_ref, other_ref)):
        holder = core ^ turned
        for position in range(4):
            line = ref[position, 128:144, :].astype(F32)[0:1]
            pair, high, mid, low = [line[:, 256 * k : 256 * k + 256] for k in range(4)]
            time = (high * 65536.0 + mid * 256.0 + low) + 1.0
            hit = pair == owner
            start = jnp.min(jnp.where(hit, row, 1e6), axis=1, keepdims=True)
            end = jnp.max(jnp.where(hit, row, -1.0), axis=1, keepdims=True)
            masks = (row == start, (row == end) & (end > start))
            source = 8 * (4 * z + y) + 2 * (x ^ distance(position, holder == 1)) + holder
            for slot, mask in enumerate(masks):
                value = jnp.sum(jnp.where(mask, time, 0.0), axis=1, keepdims=True)
                out = jnp.where(lane == PAIRS * slot + source, value, out)
    out = out.astype(jnp.int32)
    for line in range(16):
        out_ref[line] = out[line : line + 1]


def route_lists(place, own, other):
    return pl.pallas_call(
        route_kernel,
        out_shape=jax.ShapeDtypeStruct((16, 1, SLOTS), jnp.int32),
        in_specs=[SMEM, VMEM, VMEM],
        out_specs=VMEM,
        compiler_params=pltpu.CompilerParams(vmem_limit_bytes=8 * 1024 * 1024),
        cost_estimate=pl.CostEstimate(flops=1_000_000, bytes_accessed=300_000, transcendentals=0),
        name="route_lists",
    )(place, own, other)


def order_kernel(place, own_ref, other_ref, out_ref, power_ref):
    x, core = place[2], place[3]
    for turned, ref in enumerate((own_ref, other_ref)):
        holder = core ^ turned

        def one(position, carry, ref=ref, holder=holder):
            rank = 2 * (x ^ distance(position, holder == 1)) + holder
            for half in range(2):
                total = jnp.zeros((8, 128), F32)
                for part in range(2):
                    rows = pl.ds(64 * part + 32 * half, 32)
                    h = ref[position, rows, :]
                    out_ref[part, pl.ds(pl.multiple_of(64 * rank + 32 * half, 32), 32), :] = h
                    h = h.astype(F32)
                    power = h * h
                    for r in range(0, 32, 8):
                        for c in range(0, COLS, 128):
                            total = total + power[r : r + 8, c : c + 128]
                whole = jnp.sum(total, axis=(0, 1), keepdims=True)
                power_ref[pl.ds(2 * rank + half, 1), :] = jnp.broadcast_to(whole, (1, SLOTS))
            return carry

        lax.fori_loop(0, 4, one, 0)


def order_template(place, own, other):
    return pl.pallas_call(
        order_kernel,
        out_shape=(
            jax.ShapeDtypeStruct((2, ROWS, COLS), BF16),
            jax.ShapeDtypeStruct((BANDS, SLOTS), F32),
        ),
        in_specs=[SMEM, VMEM, VMEM],
        out_specs=(VMEM, VMEM),
        compiler_params=pltpu.CompilerParams(vmem_limit_bytes=12 * 1024 * 1024),
        cost_estimate=pl.CostEstimate(flops=3_000_000, bytes_accessed=4_000_000, transcendentals=0),
        name="order_template",
    )(place, own, other)


def list_masks(pair_ref, count_ref):
    shape = (PAIRS, SLOTS)
    row = lax.broadcasted_iota(jnp.int32, shape, 1).astype(F32)
    owner = lax.broadcasted_iota(jnp.int32, shape, 0)
    hit = (pair_ref[...] == owner) & (row < count_ref[0].astype(F32))
    low = jnp.min(jnp.where(hit, row, 1e6), axis=1, keepdims=True)
    high = jnp.max(jnp.where(hit, row, -1.0), axis=1, keepdims=True)
    return hit & (row == low), hit & (row == high) & (high > low)


def take_kernel(pair_ref, count_ref, back_ref, chi_ref, snr_ref):
    first, second = list_masks(pair_ref, count_ref)
    for part, out_ref in enumerate((chi_ref, snr_ref)):
        one = jnp.where(first, back_ref[:, 2 * part : 2 * part + 1], 0.0)
        two = jnp.where(second, back_ref[:, 2 * part + 1 : 2 * part + 2], 0.0)
        out_ref[...] = jnp.sum(one + two, axis=0, keepdims=True)


def take_results(pairs, counts, back):
    return pl.pallas_call(
        take_kernel,
        out_shape=(jax.ShapeDtypeStruct((1, SLOTS), F32),) * 2,
        in_specs=[VMEM, SMEM, VMEM],
        out_specs=(VMEM, VMEM),
        cost_estimate=pl.CostEstimate(flops=500_000, bytes_accessed=70_000, transcendentals=0),
        name="take_results",
    )(pairs, counts, back)


def angle_parts(numerator, modulus):
    angles = (2.0 * math.pi / modulus) * (numerator & (modulus - 1)).astype(F32)
    return jnp.cos(angles), jnp.sin(angles)


def probe_kernel(list_ref, one_ref, two_ref, shift_ref, band_ref, time_ref):
    t = jnp.sum(list_ref[...].astype(F32), axis=0, keepdims=True).astype(jnp.int32) - 1
    time_ref[...] = t
    t = jnp.maximum(t, 0)
    step = lax.broadcasted_iota(jnp.int32, (32, SLOTS), 0)
    low_r, low_i = angle_parts(step * t, BINS)
    high_r, high_i = angle_parts(step * 32 * t, BINS)
    shift_ref[0], shift_ref[1] = angle_parts(step * t, ROWS)
    band_ref[0], band_ref[1] = angle_parts(step[:BANDS] * t, BANDS)
    for h in range(32):
        hr, hi = high_r[h : h + 1], high_i[h : h + 1]
        pr = (hr * low_r - hi * low_i).astype(BF16)
        pi = (hr * low_i + hi * low_r).astype(BF16)
        rows = pl.ds(32 * h, 32)
        one_ref[rows, :SLOTS] = pr
        one_ref[rows, SLOTS:] = pi
        two_ref[rows, :SLOTS] = -pi
        two_ref[rows, SLOTS:] = pr


def probes(lists):
    return pl.pallas_call(
        probe_kernel,
        out_shape=(
            jax.ShapeDtypeStruct((COLS, 2 * SLOTS), BF16),
            jax.ShapeDtypeStruct((COLS, 2 * SLOTS), BF16),
            jax.ShapeDtypeStruct((2, 32, SLOTS), F32),
            jax.ShapeDtypeStruct((2, BANDS, SLOTS), F32),
            jax.ShapeDtypeStruct((1, SLOTS), jnp.int32),
        ),
        in_specs=[VMEM],
        out_specs=(VMEM,) * 5,
        compiler_params=pltpu.CompilerParams(vmem_limit_bytes=LIMIT),
        cost_estimate=pl.CostEstimate(flops=4_000_000, bytes_accessed=2_200_000, transcendentals=60_000),
        name="probes",
    )(lists)


def block_place(place, det, late, early):
    z, y, core = place[0], place[1], place[3]
    late, early = distance(late, core == 1), distance(early, core == 1)
    return (z ^ late, y ^ early) if det == 0 else (z ^ early, y ^ late)


def spectra_kernel(half, place, template_ref, part0, part1, spec):
    for det, part in enumerate((part0, part1)):

        def one_block(m, carry, det=det, part=part):
            zz, yy = block_place(place, det, 2 * half + (m >> 2), m & 3)
            rows = pl.ds(pl.multiple_of(128 * zz + 32 * yy, 32), 32)
            for lane in range(0, COLS, 256):
                cols = pl.ds(lane, 256)
                hr = template_ref[0, rows, cols].astype(F32)
                hi = template_ref[1, rows, cols].astype(F32)
                xr = part[m, 0, :, cols].astype(F32)
                xi = part[m, 1, :, cols].astype(F32)
                spec[0, 8 * det + m, :, cols] = (hr * xr + hi * xi).astype(BF16)
                spec[1, 8 * det + m, :, cols] = (hr * xi - hi * xr).astype(BF16)
            return carry

        lax.fori_loop(0, 8, one_block, 0, unroll=2)


def spectra(half, place, template, parts):
    return pl.pallas_call(
        functools.partial(spectra_kernel, half),
        out_shape=jax.ShapeDtypeStruct((2, 16, 32, COLS), BF16),
        in_specs=[SMEM, VMEM, VMEM, VMEM],
        out_specs=VMEM,
        compiler_params=pltpu.CompilerParams(vmem_limit_bytes=12 * 1024 * 1024),
        cost_estimate=pl.CostEstimate(flops=3_000_000, bytes_accessed=6_000_000, transcendentals=0),
        name=("spectra_early", "spectra_late")[half],
    )(place, template, *parts)


def veto_kernel(place, power_ref, time_ref, one_ref, two_ref, shift_ref, band_ref, s0, s1, result_ref, sum_ref):
    sr, si = shift_ref[0], shift_ref[1]
    for half, spec in enumerate((s0, s1)):
        out = jnp.dot(spec[0].reshape(512, COLS), one_ref[...], preferred_element_type=F32)
        out = out + jnp.dot(spec[1].reshape(512, COLS), two_ref[...], preferred_element_type=F32)
        for det in range(2):
            for m in range(8):
                i = 8 * det + m
                yr = out[32 * i : 32 * i + 32, :SLOTS]
                yi = out[32 * i : 32 * i + 32, SLOTS:]
                ar = jnp.sum(yr * sr - yi * si, axis=0, keepdims=True)
                ai = jnp.sum(yr * si + yi * sr, axis=0, keepdims=True)
                zz, yy = block_place(place, det, 2 * half + (m >> 2), m & 3)
                band = 4 * zz + yy
                er = band_ref[0, pl.ds(band, 1), :]
                ei = band_ref[1, pl.ds(band, 1), :]
                sum_ref[pl.ds(BANDS * det + band, 1), :SLOTS] = ar * er - ai * ei
                sum_ref[pl.ds(BANDS * det + band, 1), SLOTS:] = ar * ei + ai * er
    power = power_ref[...]
    sigma = jnp.sum(power, axis=0, keepdims=True)
    weight = power / sigma
    chi = jnp.zeros((1, SLOTS), F32)
    snr = jnp.zeros((1, SLOTS), F32)
    for det in range(2):
        rows = pl.ds(BANDS * det, BANDS)
        br, bi = sum_ref[rows, :SLOTS], sum_ref[rows, SLOTS:]
        tr = jnp.sum(br, axis=0, keepdims=True)
        ti = jnp.sum(bi, axis=0, keepdims=True)
        dr = br - weight * tr
        di = bi - weight * ti
        chi = chi + jnp.sum((dr * dr + di * di) / (weight * sigma), axis=0, keepdims=True)
        snr = snr + (tr * tr + ti * ti)
    usable = time_ref[...] >= 0
    chi = jnp.where(usable, chi / (4.0 * (BANDS - 1)), 0.0)
    snr = jnp.where(usable, snr / (2.0 * sigma), 0.0)
    lines = [chi[:, :128], chi[:, 128:], snr[:, :128], snr[:, 128:], sigma[:, :128], jnp.zeros((123, 128), F32)]
    result_ref[...] = jnp.concatenate(lines, axis=0).T


def veto(place, power, times, tables, specs):
    return pl.pallas_call(
        veto_kernel,
        out_shape=jax.ShapeDtypeStruct((PAIRS, 128), F32),
        in_specs=[SMEM] + [VMEM] * 8,
        out_specs=VMEM,
        scratch_shapes=[pltpu.VMEM((2 * BANDS, 2 * SLOTS), F32)],
        compiler_params=pltpu.CompilerParams(vmem_limit_bytes=20 * 1024 * 1024),
        cost_estimate=pl.CostEstimate(
            flops=2_200_000_000, bytes_accessed=6_000_000, transcendentals=0
        ),
        name="veto",
    )(place, power, times, *tables, *specs)


def series_kernel(
    place, s0_hbm, s1_hbm, result_hbm, rows_hbm, turn_hbm, cols_hbm, out_hbm, peak_ref,
    s0, s1, sigma_ref, rows_ref, turn_ref, cols_ref, x_ref, g_ref, w_ref, v_ref, t_ref, o_ref, sems,
):
    copies = [
        pltpu.make_async_copy(src, dst, sems.at[k])
        for k, (src, dst) in enumerate(
            (
                (s0_hbm.at[:, :8], s0.at[:, :8]),
                (s1_hbm.at[:, :8], s1.at[:, :8]),
                (s0_hbm.at[:, 8:], s0.at[:, 8:]),
                (s1_hbm.at[:, 8:], s1.at[:, 8:]),
                *[
                    pair
                    for p in range(4)
                    for pair in (
                        (rows_hbm.at[p], rows_ref.at[p]),
                        (turn_hbm.at[p], turn_ref.at[p]),
                    )
                ],
                (cols_hbm, cols_ref),
                (result_hbm.at[:8], sigma_ref),
            )
        )
    ]
    for copy in copies:
        copy.start()
    specs = (s0, s1)
    z, y, core = place[0], place[1], place[3]

    def four(q):
        (r0, i0), (r1, i1), (r2, i2), (r3, i3) = q
        ar, ai = r0 + r2, i0 + i2
        br, bi = r1 + r3, i1 + i3
        cr, ci = r0 - r2, i0 - i2
        dr, di = r1 - r3, i1 - i3
        return (
            (ar + br, ai + bi),
            (cr - di, ci + dr),
            (ar - br, ai - bi),
            (cr + di, ci - dr),
        )

    turned = ((z & 1) ^ core) == 1

    def fold(det, yy, load):
        def chunk(k, carry):
            cols = pl.ds(pl.multiple_of(k * 256, 256), 256)
            q = [(load(o, 0, cols).astype(F32), load(o, 1, cols).astype(F32)) for o in (0, 1, 3, 2)]
            for p, (re, im) in enumerate(four(q)):
                to = jnp.where(turned, (4 - p) & 3, p)
                x_ref[det, to, pl.ds(pl.multiple_of(32 * yy, 32), 32), cols] = re.astype(BF16)
                x_ref[det, to, pl.ds(pl.multiple_of(128 + 32 * yy, 32), 32), cols] = im.astype(BF16)
            return carry

        lax.fori_loop(0, 4, chunk, 0)

    for det in range(2):
        copies[2 * det].wait()
        copies[2 * det + 1].wait()

        for m in range(4):
            if det == 0:
                load = lambda o, k, cols: specs[o >> 1][k, 4 * (o & 1) + m, :, cols]
            else:
                load = lambda o, k, cols: specs[m >> 1][k, 8 + 4 * (m & 1) + o, :, cols]
            fold(det, y ^ distance(m, core == 1), load)

    def first(step):
        p, det = divmod(step, 2)
        if det == 0:
            copies[4 + 2 * p].wait()
            copies[5 + 2 * p].wait()
        for j in range(4):
            cols = pl.ds(256 * j, 256)
            g_ref[step % 2, :, cols] = jnp.dot(
                rows_ref[p, j], x_ref[det, p, :, cols], preferred_element_type=F32
            )

    def turn(step):
        p, det = divmod(step, 2)
        for r in range(0, 128, 16):
            h = []
            for j in range(4):
                cols = pl.ds(256 * j, 256)
                h.append((g_ref[step % 2, pl.ds(r, 16), cols], g_ref[step % 2, pl.ds(128 + r, 16), cols]))
            tr = turn_ref[p, 0, pl.ds(r, 16), :]
            ti = turn_ref[p, 1, pl.ds(r, 16), :]
            rows = pl.ds(128 * p + r, 16)
            for k, (re, im) in enumerate(four(h)):
                w_ref[k, det, rows, :256] = (re * tr - im * ti).astype(BF16)
                w_ref[k, det, rows, 256:] = (re * ti + im * tr).astype(BF16)

    first(0)
    for step in range(8):
        if step < 7:
            first(step + 1)
        turn(step)
    copies[12].wait()
    copies[13].wait()

    scale = 1.0 / (2.0 * sigma_ref[0, 4])

    def second(k):
        for det in range(2):
            v_ref[k % 2, det] = jnp.dot(w_ref[k, det], cols_ref[k], preferred_element_type=F32)

    def power(k, best):
        for p in range(4):
            for r in range(0, 128, 16):
                rows = pl.ds(128 * p + r, 16)
                v = [
                    v_ref[k % 2, det, rows, pl.ds(256 * part, 256)]
                    for det in range(2)
                    for part in range(2)
                ]
                total = (v[0] * v[0] + v[1] * v[1] + v[2] * v[2] + v[3] * v[3]) * scale
                best = jnp.maximum(best, jnp.maximum(total[:8], total[8:]))
                for half in range(2):
                    t_ref[2 * k + half, pl.ds(4 * r + p, 16, stride=4), :] = total[
                        :, 128 * half : 128 * half + 128
                    ]
        return best

    best = jnp.zeros((8, 256), F32)
    second(0)
    for k in range(4):
        if k < 3:
            second(k + 1)
        best = power(k, best)
    peak_ref[...] = jnp.max(best, axis=(0, 1), keepdims=True)
    for i in range(4):
        for k in range(4):
            for half in range(2):
                tile = t_ref[2 * k + half, pl.ds(128 * i, 128), :]
                o_ref[i, pl.ds(512 * half + k, 128, stride=4), :] = tile.T
        copy = pltpu.make_async_copy(
            o_ref.at[i], out_hbm.at[:, pl.ds(128 * i, 128)], sems.at[14 + i]
        )
        copy.start()
        copies.append(copy)
    for copy in copies[14:]:
        copy.wait()


def series(place, specs, result, rows, turns, cols):
    hbm = pl.BlockSpec(memory_space=pltpu.HBM)
    return pl.pallas_call(
        series_kernel,
        out_shape=(
            jax.ShapeDtypeStruct((COLS, ROWS), F32),
            jax.ShapeDtypeStruct((1, 1), F32),
        ),
        in_specs=[SMEM] + [hbm] * 6,
        out_specs=(hbm, VMEM),
        scratch_shapes=[
            pltpu.VMEM(specs[0].shape, BF16),
            pltpu.VMEM(specs[1].shape, BF16),
            pltpu.VMEM((8, 128), F32),
            pltpu.VMEM(rows.shape, rows.dtype),
            pltpu.VMEM(turns.shape, turns.dtype),
            pltpu.VMEM(cols.shape, cols.dtype),
            pltpu.VMEM((2, 4, 256, COLS), BF16),
            pltpu.VMEM((2, 256, COLS), F32),
            pltpu.VMEM((4, 2, ROWS, 512), BF16),
            pltpu.VMEM((2, 2, ROWS, 512), F32),
            pltpu.VMEM((8, ROWS, 128), F32),
            pltpu.VMEM((4, COLS, 128), F32),
            pltpu.SemaphoreType.DMA((18,)),
        ],
        compiler_params=pltpu.CompilerParams(vmem_limit_bytes=60 * 1024 * 1024),
        cost_estimate=pl.CostEstimate(
            flops=3_300_000_000, bytes_accessed=13_000_000, transcendentals=0
        ),
        name="series",
    )(place, *specs, result, rows, turns, cols)


def shards(strain, templates, trig_pair, trig_time, trig_counts):
    device = lax.axis_index("tmpl")
    seat = lax.axis_index("seg")
    place = jnp.stack([device // 4, device % 4, seat // 2, seat % 2]).astype(jnp.int32)

    a, b, t = pack_lists(strain, templates[:, 0], trig_pair, trig_time, trig_counts)
    for step, (near, far) in enumerate(((1, 3), (3, 1), (1, 3), (3, 1))):
        more_a = swap(a, ("yyzz"[step], near), ("yyzz"[step], far))
        more_b = swap(b, ("zzyy"[step], near), ("zzyy"[step], far))
        if step < 2:
            t = jnp.concatenate([t, swap(t, ("x", near), ("x", far))])
        if step < 3:
            a, b = jnp.concatenate([a, more_a]), jnp.concatenate([b, more_b])
    other_t = swap(t, ("core", 1), ("core", 1))

    outgoing = route_lists(place, t, other_t)
    incoming = lax.all_to_all(outgoing, "tmpl", split_axis=0, concat_axis=0, tiled=True)
    template, power = order_template(place, t, other_t)
    more_a, more_b, incoming = lax.optimization_barrier((more_a, more_b, incoming))
    specs = spectra(0, place, template, (a, b)), spectra(1, place, template, (more_a, more_b))
    *tables, times = probes(incoming.reshape(16, SLOTS))
    result = veto(place, power, times, tables, specs)
    back = lax.all_to_all(result, ("tmpl", "seg"), split_axis=0, concat_axis=0, tiled=True)
    snr_series, peak = series(
        place,
        specs,
        result,
        jnp.asarray(row_matrices()),
        jnp.asarray(twiddles()),
        jnp.asarray(col_matrices()),
    )
    chi, snr = take_results(trig_pair, trig_counts, back)
    return (snr_series[None, None], peak, chi, snr)


def solution(mesh):
    in_specs = (
        P(None, None, "seg", "tmpl", None),
        P(None, "tmpl", "seg", None),
        P(("tmpl", "seg"), None),
        P(("tmpl", "seg"), None),
        P(("tmpl", "seg")),
    )
    out_specs = (
        P("tmpl", "seg", None, None),
        P("tmpl", "seg"),
        P(("tmpl", "seg"), None),
        P(("tmpl", "seg"), None),
    )
    return jax.shard_map(shards, mesh=mesh, in_specs=in_specs, out_specs=out_specs, check_vma=False)
```
